256 devices in a mesh: grp: 4 (over z_hi), gx: 32 (over x, z_lo, y), gy: 2 (over core).
Axes of the slice: x: 4, y: 4, z: 8 (z_hi: 4, z_lo: 2; z = z_hi * 2 + z_lo), core: 2. Of those that a mesh axis runs over, the one named last changes fastest.
Arguments:
- fluid_temp: float32 [512, 256, 1024], P('gx', 'gy', 'grp'), may hold values from -6 to 6
- active: int32 [512, 256, 1024], P('gx', 'gy', 'grp'), may hold values 0 or 1
- fin_temp: float32 [256, 1024, 512], P('grp', 'gx', 'gy'), may hold values from -6 to 6
- fin_source: float32 [256, 1024, 512], P('grp', 'gx', 'gy'), may hold values from -6 to 6
- wall_owner: int32 [32, 2, 2048, 1], P('gx', 'gy'), may hold values from 0 to 31, as said below
- wall_target: int32 [32, 2, 2048], P('gx', 'gy'), may hold values from 0 to 8191, as said below
Outputs:
- fluid_new: float32 [512, 256, 1024], P('gx', 'gy', 'grp')
- fin_new: float32 [256, 1024, 512], P('grp', 'gx', 'gy')
The draws below stay inside these ranges and needn't reach their ends.
Inputs may be any that keep to these rules, and one draw needn't show every extreme that they name: `wall_owner`: among the 2048 wall cells of one column block (a, b), exactly 128 name the owner a and at most 128 name any one owner; in every draw one owner is named by exactly 128 wall cells of every column block. `wall_target`: wall cell w = i * 128 + j names a root cell (2 * i + di) * 256 + 2 * j + dj of the 2 x 2 patch beneath it, di and dj being 0 or 1; the first wall cell of a block names its patch's first root cell, the last one its patch's last.
All inputs are finite; a program needn't handle non-finite values. No bound on the sum of `active` on one device may be relied on, other than what follows from the above.
Results may differ from the reference program's by a relative error of at most 0.00002.
Values sent between devices are 32-bit elements; how exact they have to be, the bound alone decides.
A program may use at most 64 MiB of HBM per device.

```python
import jax
import jax.numpy as jnp
from jax import lax

CX = 16
CY = 128
FW = 32
FH = 256
NX = 512
NY = 256
NZ = 1024
FZG = 256
FWG = 1024
FHG = 512
CAP = 128
N_GX = 32
N_GY = 2


def owner_block(block_key, home, star):
    wall_cells = CX * CY
    away_count = (N_GX - 1) * CAP
    first_key, second_key = jax.random.split(block_key)
    order = jax.random.permutation(first_key, wall_cells)
    slot_scores = jax.random.permutation(second_key, away_count)
    slot_owner = (home + jnp.arange(away_count, dtype=jnp.int32) // CAP + 1) % N_GX
    priority = jnp.where(slot_owner == star, 0, away_count) + slot_scores
    slot_order = jnp.argsort(priority, stable=True)
    ranks = jnp.arange(wall_cells, dtype=jnp.int32)
    picked = slot_order[jnp.clip(ranks - CAP, 0, away_count - 1)]
    by_rank = jnp.where(ranks < CAP, home, slot_owner[picked]).astype(jnp.int32)
    return jnp.zeros((wall_cells,), jnp.int32).at[order].set(by_rank)


def draw_wall_owner(key, part):
    base = jax.random.fold_in(key, 11)
    star = jax.random.randint(jax.random.fold_in(base, 7), (), 0, N_GX).astype(jnp.int32)
    block_ids = jnp.arange(N_GX * N_GY, dtype=jnp.int32)
    homes = block_ids // N_GY
    keys = jax.vmap(lambda ident: jax.random.fold_in(base, ident))(block_ids)
    owners = jax.vmap(lambda block_key, home: owner_block(block_key, home, star))(keys, homes)
    return owners.reshape(N_GX, N_GY, CX * CY, 1)


def draw_wall_target(key, part):
    base = jax.random.fold_in(key, 23)
    wall_cells = CX * CY
    shifts = jax.random.randint(base, (N_GX, N_GY, wall_cells, 2), 0, 2).astype(jnp.int32)
    cells = jnp.arange(wall_cells, dtype=jnp.int32)
    row_shift = jnp.where(cells == 0, 0, jnp.where(cells == wall_cells - 1, 1, shifts[..., 0]))
    col_shift = jnp.where(cells == 0, 0, jnp.where(cells == wall_cells - 1, 1, shifts[..., 1]))
    rows = cells // CY
    columns = cells % CY
    return ((2 * rows + row_shift) * FH + 2 * columns + col_shift).astype(jnp.int32)


def plant(array, own_key, least, high):
    dims = array.shape
    index_at = [jax.random.randint(jax.random.fold_in(own_key, axis), (), 0, dims[axis]) for axis in range(len(dims))]
    array = array.at[tuple(index_at)].set(least)
    longest = dims.index(max(dims))
    index_at[longest] = (index_at[longest] + 1) % dims[longest]
    return array.at[tuple(index_at)].set(high)


def block_scale(stream_key, shape, cuts, smallest, largest):
    def one(axis_at, blocks):
        draws = jax.random.uniform(jax.random.fold_in(jax.random.fold_in(stream_key, 6), axis_at), (blocks,), jnp.float32, smallest / len(cuts), largest / len(cuts))
        return jnp.repeat(jnp.exp(draws), shape[axis_at] // blocks).reshape((-1,) + (1,) * (len(shape) - axis_at - 1))

    level = one(*cuts[0])
    for cut in cuts[1:]:
        level = level * one(*cut)
    return level


def centred(key, extent, deviation, most, cuts=(), kind=jnp.bfloat16):
    factor_of = block_scale(key, extent, cuts, -0.22, 0.18) if cuts else 1.0
    drawn = jax.random.normal(key, extent, jnp.float32) * deviation * factor_of
    return jnp.minimum(jnp.maximum(drawn, -most), most).astype(kind)


def setup_inputs(seed: int = 0) -> dict:
    streams_of = jax.random.split(jax.random.key(seed), 7)
    return {
        "fluid_temp": centred(streams_of[0], (NX, NY, NZ), 1.0, 6.0, ((0, 32), (1, 2), (2, 4)), jnp.float32),
        "active": plant((jax.random.randint(streams_of[1], (NX, NY, NZ), 0, 8) < 7).astype(jnp.int32), jax.random.fold_in(streams_of[1], 1), 0, 1),
        "fin_temp": centred(streams_of[2], (FZG, FWG, FHG), 1.0, 6.0, ((0, 4), (1, 32), (2, 2)), jnp.float32),
        "fin_source": centred(streams_of[3], (FZG, FWG, FHG), 1.0, 6.0, ((0, 4), (1, 32), (2, 2)), jnp.float32),
        "wall_owner": draw_wall_owner(jax.random.fold_in(streams_of[6], 71), 0),
        "wall_target": draw_wall_target(jax.random.fold_in(streams_of[6], 71), 0),
    }


FLUID_DIFFUSION = 1.0
FIN_CONDUCTION = 1.0
HEAT_COEF = 1.0


def six_sum(padded):
    return (padded[2:, 1:-1, 1:-1] + padded[:-2, 1:-1, 1:-1] + padded[1:-1, 2:, 1:-1]
            + padded[1:-1, :-2, 1:-1] + padded[1:-1, 1:-1, 2:] + padded[1:-1, 1:-1, :-2])


def fin_image(field):
    padded = jnp.pad(field, 1)
    return (1.0 + 6.0 * FIN_CONDUCTION) * field - FIN_CONDUCTION * six_sum(padded)


def reference(fluid_temp, active, fin_temp, fin_source, wall_owner, wall_target):
    owners = wall_owner[..., 0]
    column_b = lax.broadcasted_iota(jnp.int32, owners.shape, 1)
    surf_first = owners * FW + wall_target // FH
    surf_second = column_b * FH + wall_target % FH
    surface_index = (surf_first * FHG + surf_second).astype(jnp.int32)
    surface = fin_temp[0].reshape(-1)
    fin_wall = surface[surface_index]
    bottom = fluid_temp[:, :, 0].reshape(N_GX, CX, N_GY, CY).transpose(0, 2, 1, 3).reshape(N_GX, N_GY, CX * CY)
    heat_flux = HEAT_COEF * (bottom - fin_wall)
    deposit = jax.ops.segment_sum(heat_flux.reshape(-1), surface_index.reshape(-1), num_segments=FWG * FHG)
    fin_rhs = fin_temp + fin_source
    fin_rhs = fin_rhs.at[0].add(deposit.reshape(FWG, FHG))
    diag = 1.0 + 6.0 * FIN_CONDUCTION
    spectral = 6.0 * FIN_CONDUCTION / diag
    omega = 1.0 / (1.0 - spectral * spectral / 2.0)
    first_state = fin_temp + (fin_rhs - fin_image(fin_temp)) / diag
    fin_new = omega * (first_state + (fin_rhs - fin_image(first_state)) / diag - fin_temp) + fin_temp

    ghost = fin_wall.reshape(N_GX, N_GY, CX, CY).transpose(0, 2, 1, 3).reshape(NX, NY)
    shape = fluid_temp.shape
    colour = (lax.broadcasted_iota(jnp.int32, shape, 0) + lax.broadcasted_iota(jnp.int32, shape, 1)
              + lax.broadcasted_iota(jnp.int32, shape, 2)) % 2
    red_mask = (colour == 0) & (active == 1)
    black_mask = (colour == 1) & (active == 1)

    def half_sweep(field, update_mask):
        padded = jnp.pad(field, 1)
        padded = padded.at[1:-1, 1:-1, 0].set(ghost)
        updated = (fluid_temp + FLUID_DIFFUSION * six_sum(padded)) / (1.0 + 6.0 * FLUID_DIFFUSION)
        return jnp.where(update_mask, updated, field)

    red_temp = half_sweep(fluid_temp, red_mask)
    fluid_new = half_sweep(red_temp, black_mask)
    return fluid_new, fin_new
```

```python
import functools

import jax
import jax.numpy as jnp
from jax import lax
from jax.experimental import pallas as pl
from jax.experimental.pallas import tpu as pltpu
from jax.sharding import PartitionSpec as P

F32 = jnp.float32
MESH = pl.DeviceIdType.MESH
DIAG = 7.0
SPECTRAL = 6.0 / DIAG
OMEGA = 1.0 / (1.0 - SPECTRAL * SPECTRAL / 2.0)
SEVENTH = 1.0 / 7.0

CX, CY, CZ = 16, 128, 256
FD, FW, FH = 64, 32, 256
ROWS = CX

FLUID_UP, FLUID_DOWN, FLUID_SIDE, FLUID_ABOVE, FLUID_BELOW = 0, 1, 2, 3, 4
FIN_UP, FIN_DOWN, FIN_SIDE, FIN_ABOVE, FIN_BELOW = 5, 6, 7, 8, 9
FACES = 10


def iota(shape, axis):
    return lax.broadcasted_iota(jnp.int32, shape, axis)


def parity_rows(shape):
    rows, lanes = shape
    tile = (iota((8, lanes), 0) + iota((8, lanes), 1)) % 2
    return jnp.concatenate([tile] * (rows // 8), axis=0)


def shifted_rows(plane, low_tile, high_tile):
    rows, lanes = plane.shape
    sub = iota((8, lanes), 0)
    up = pltpu.roll(plane, 1, 0)
    down = pltpu.roll(plane, rows - 1, 0)
    up = jnp.concatenate([jnp.where(sub == 0, low_tile, up[:8]), up[8:]], axis=0)
    down = jnp.concatenate([down[:-8], jnp.where(sub == 7, high_tile, down[-8:])], axis=0)
    return up + down


def shifted_lanes(plane, low_tile, high_tile):
    rows, lanes = plane.shape
    lane = iota((rows, 128), 1)
    left = pltpu.roll(plane, 1, 1)
    right = pltpu.roll(plane, lanes - 1, 1)
    first = jnp.where(lane == 0, low_tile, left[:, :128]) + right[:, :128]
    last = left[:, 128:] + jnp.where(lane == 127, high_tile, right[:, 128:])
    return jnp.concatenate([first, last], axis=1)


def fluid_plane(x, field, active, side, low, high, parity, core):
    here = field[x + 1]
    total = field[x] + field[x + 2]
    tile = side[x]
    low_tile = jnp.where(core == 1, pltpu.roll(tile, 1, 0), 0.0)
    high_tile = jnp.where(core == 0, pltpu.roll(tile, 7, 0), 0.0)
    total = total + shifted_rows(here, low_tile, high_tile)
    low_lane = pltpu.roll(low[...], (128 - x) % 128, 1)
    high_lane = pltpu.roll(high[...], 127 - x, 1)
    total = total + shifted_lanes(here, low_lane, high_lane)
    on = jnp.where(parity_rows(here.shape) == (x + parity) % 2, active[x], 0) == 1
    return jnp.where(on, (here + total) * SEVENTH, here)


def fin_sum(group, k, field, low, high, side, core):
    d = group * 8 + k
    here = field[d + 1]
    total = field[d] + field[d + 2]
    low_tile = pltpu.roll(low[group], (8 - k) % 8, 0)
    high_tile = pltpu.roll(high[group], 7 - k, 0)
    total = total + shifted_rows(here, low_tile, high_tile)
    column = pltpu.roll(side[...], jnp.where(core == 1, (128 - d) % 128, 127 - d), 1)
    total = total + shifted_lanes(
        here, jnp.where(core == 1, column, 0.0), jnp.where(core == 0, column, 0.0)
    )
    return here, total


def pick_columns(x, plane, low, high):
    lane = iota((plane.shape[0], 128), 1)
    low[...] = jnp.where(lane == x, pltpu.roll(plane[:, :128], x, 1), low[...])
    high[...] = jnp.where(lane == x, pltpu.roll(plane[:, 128:], (x + 1) % 128, 1), high[...])


def pick_rows(k, plane, low, high):
    sub = iota((8, plane.shape[1]), 0)
    low = jnp.where(sub == k, pltpu.roll(plane[:8], k, 0), low)
    high = jnp.where(sub == k, pltpu.roll(plane[-8:], (k + 1) % 8, 0), high)
    return low, high


def pick_side(d, plane, out, core):
    lane = iota((plane.shape[0], 128), 1)
    half = jnp.where(core == 0, plane[:, 128:], plane[:, :128])
    turned = pltpu.roll(half, jnp.where(core == 0, (d + 1) % 128, d), 1)
    out[...] = jnp.where(lane == d, turned, out[...])


def spread(rows, columns, offset, axis):
    a, b = iota((rows, columns), axis), iota((rows, columns), 1 - axis)
    return jnp.where(a == 2 * b + offset, 1.0, 0.0).astype(F32)


def dot(a, b):
    return jnp.dot(a, b, precision=lax.Precision.HIGHEST, preferred_element_type=F32)


def exchange_kernel(
    sizes,
    fluid, active, fin, source, owner, target,
    red, active_v, first, base, side2, low2, high2, fin_low2, fin_high2, fin_side2,
    fluid_v, fin_v, source_v, owner_v, target_v,
    side1, low1, high1, fin_low1, fin_high1, fin_side1,
    out_low1, out_high1, out_fin_low1, out_fin_high1, out_fin_side1,
    out_low2, out_high2, out_fin_low2, out_fin_high2, out_fin_side2,
    wall_out, wall_in, back_out, back_in,
    load_sem, send1, recv1, send2, recv2, wall_send, wall_recv, back_send, back_recv,
):
    groups, blocks = sizes
    grp, gx, core = lax.axis_index("grp"), lax.axis_index("gx"), lax.axis_index("gy")
    has_low, has_high = gx > 0, gx < blocks - 1
    has_below, has_above = grp > 0, grp < groups - 1
    on_wall = grp == 0
    left, right = (grp, gx - 1, core), (grp, gx + 1, core)
    below, above = (grp - 1, gx, core), (grp + 1, gx, core)
    other = (grp, gx, 1 - core)

    def peer(k):
        return (grp, lax.rem(gx + k, blocks), core)

    def peer_back(k):
        return (grp, lax.rem(gx - k + blocks, blocks), core)

    loads = [
        pltpu.make_async_copy(owner, owner_v, load_sem.at[0]),
        pltpu.make_async_copy(target, target_v, load_sem.at[1]),
        pltpu.make_async_copy(fluid, fluid_v.at[pl.ds(1, CX)], load_sem.at[2]),
        pltpu.make_async_copy(fin, fin_v.at[pl.ds(1, FD)], load_sem.at[3]),
        pltpu.make_async_copy(active, active_v, load_sem.at[4]),
        pltpu.make_async_copy(source, source_v, load_sem.at[5]),
    ]
    for load in loads:
        load.start()

    barrier = pltpu.get_barrier_semaphore()

    def greet(device):
        pl.semaphore_signal(barrier, inc=1, device_id=device, device_id_type=MESH)

    greet(other)

    @pl.when(has_above)
    def _():
        greet(above)

    @pl.when(has_below)
    def _():
        greet(below)

    @pl.when(on_wall)
    def _():
        def step(k, carry):
            greet(peer(k))
            return carry

        lax.fori_loop(1, blocks, step, 0)

    @pl.when(jnp.logical_not(on_wall) & has_low)
    def _():
        greet(left)

    @pl.when(jnp.logical_not(on_wall) & has_high)
    def _():
        greet(right)

    @pl.when(jnp.logical_not(has_low))
    def _():
        fluid_v[0] = jnp.zeros((CY, CZ), F32)
        red[0] = jnp.zeros((CY, CZ), F32)
        fin_low1[...] = jnp.zeros(fin_low1.shape, F32)
        fin_low2[...] = jnp.zeros(fin_low2.shape, F32)

    @pl.when(jnp.logical_not(has_high))
    def _():
        fluid_v[CX + 1] = jnp.zeros((CY, CZ), F32)
        red[CX + 1] = jnp.zeros((CY, CZ), F32)
        fin_high1[...] = jnp.zeros(fin_high1.shape, F32)
        fin_high2[...] = jnp.zeros(fin_high2.shape, F32)

    @pl.when(jnp.logical_not(has_below))
    def _():
        low1[...] = jnp.zeros(low1.shape, F32)

    @pl.when(jnp.logical_not(has_above))
    def _():
        high1[...] = jnp.zeros(high1.shape, F32)
        high2[...] = jnp.zeros(high2.shape, F32)
        fin_v[FD + 1] = jnp.zeros((FW, FH), F32)
        first[FD + 1] = jnp.zeros((FW, FH), F32)

    for ref in (out_low1, out_high1, out_fin_side1, out_low2, out_high2, out_fin_side2):
        ref[...] = jnp.zeros(ref.shape, F32)

    loads[0].wait()
    loads[1].wait()
    loads[2].wait()

    def pack_fluid(x, carry):
        pick_columns(x, fluid_v[x + 1], out_low1, out_high1)
        return carry

    lax.fori_loop(0, CX, pack_fluid, 0)

    expected = 1 + has_above.astype(jnp.int32) + has_below.astype(jnp.int32)
    sides = has_low.astype(jnp.int32) + has_high.astype(jnp.int32)
    pl.semaphore_wait(barrier, expected + jnp.where(on_wall, blocks - 1, sides))

    def link(src, dst, send, recv, k, device):
        return pltpu.make_async_remote_copy(
            src_ref=src, dst_ref=dst, send_sem=send.at[k], recv_sem=recv.at[k],
            device_id=device, device_id_type=MESH,
        )

    def wall_link(k):
        return link(wall_out.at[k], wall_in.at[k], wall_send, wall_recv, k, peer(k))

    def back_link(k):
        return link(back_out.at[k], back_in.at[k], back_send, back_recv, k, peer_back(k))

    @pl.when(on_wall)
    def _():
        temps = jnp.transpose(out_low1[...])[:ROWS]
        owners = owner_v[...]
        targets = target_v[...].astype(F32)

        def masked(k, out):
            out[k, :ROWS] = temps
            out[k, ROWS:] = jnp.where(owners == lax.rem(gx + k, blocks), targets, -1.0)

        def step(k, carry):
            masked(k, wall_out)
            wall_link(k).start()
            return carry

        masked(0, wall_in)
        lax.fori_loop(1, blocks, step, 0)

    side_row = pl.multiple_of(jnp.where(core == 0, CY - 8, 0), 8)

    def faces(send, recv, fluid_from, fluid_off, fluid_to, side, low, high, sent_low, sent_high,
              fin_from, fin_off, fin_to, fin_low, fin_high, fin_side, sent_fin_low, sent_fin_high, sent_fin_side):
        return {
            FLUID_UP: (link(fluid_from.at[CX - 1 + fluid_off], fluid_to.at[0], send, recv, FLUID_UP, right), has_high, has_low),
            FLUID_DOWN: (link(fluid_from.at[fluid_off], fluid_to.at[CX + 1], send, recv, FLUID_DOWN, left), has_low, has_high),
            FLUID_SIDE: (link(fluid_from.at[pl.ds(fluid_off, CX), pl.ds(side_row, 8)], side, send, recv, FLUID_SIDE, other), None, None),
            FLUID_ABOVE: (link(sent_high, low, send, recv, FLUID_ABOVE, above), has_above, has_below),
            FLUID_BELOW: (link(sent_low, high, send, recv, FLUID_BELOW, below), has_below, has_above),
            FIN_UP: (link(sent_fin_high, fin_low, send, recv, FIN_UP, right), has_high, has_low),
            FIN_DOWN: (link(sent_fin_low, fin_high, send, recv, FIN_DOWN, left), has_low, has_high),
            FIN_SIDE: (link(sent_fin_side, fin_side, send, recv, FIN_SIDE, other), None, None),
            FIN_ABOVE: (link(fin_from.at[FD - 1 + fin_off], fin_to.at[0], send, recv, FIN_ABOVE, above), has_above, has_below),
            FIN_BELOW: (link(fin_from.at[fin_off], fin_to.at[FD + 1], send, recv, FIN_BELOW, below), has_below, has_above),
        }

    def when(condition, action):
        if condition is None:
            action()
        else:
            pl.when(condition)(action)

    one = faces(send1, recv1, fluid, 0, fluid_v, side1, low1, high1, out_low1, out_high1,
                fin, 0, fin_v, fin_low1, fin_high1, fin_side1, out_fin_low1, out_fin_high1, out_fin_side1)
    two = faces(send2, recv2, red, 1, red, side2, low2, high2, out_low2, out_high2,
                first, 1, first, fin_low2, fin_high2, fin_side2, out_fin_low2, out_fin_high2, out_fin_side2)

    def start(links, *which):
        for k in which:
            when(links[k][1], links[k][0].start)

    def arrived(links, *which):
        for k in which:
            when(links[k][2], links[k][0].wait_recv)

    def sent(links):
        for k in range(FACES):
            when(links[k][1], links[k][0].wait_send)

    start(one, FLUID_SIDE, FLUID_ABOVE, FLUID_BELOW, FIN_ABOVE, FIN_BELOW, FLUID_UP, FLUID_DOWN)

    loads[3].wait()

    def pack_fin(group, carry):
        low = high = jnp.zeros((8, FH), F32)
        for k in range(8):
            plane = fin_v[group * 8 + k + 1]
            low, high = pick_rows(k, plane, low, high)
            pick_side(group * 8 + k, plane, out_fin_side1, core)
        out_fin_low1[group] = low
        out_fin_high1[group] = high
        return carry

    lax.fori_loop(0, FD // 8, pack_fin, 0)
    start(one, FIN_SIDE, FIN_UP, FIN_DOWN)

    loads[4].wait()
    loads[5].wait()
    arrived(one, FLUID_SIDE, FLUID_ABOVE, FLUID_BELOW)

    def red_step(x, carry):
        new = fluid_plane(x, fluid_v, active_v, side1, low1, high1, 0, core)
        red[x + 1] = new
        pick_columns(x, new, out_low2, out_high2)
        return carry

    lax.fori_loop(1, CX - 1, red_step, 0)
    arrived(one, FLUID_UP, FLUID_DOWN)
    red_step(0, 0)
    red_step(CX - 1, 0)

    arrived(one, FIN_SIDE, FIN_UP, FIN_DOWN, FIN_BELOW)

    def fin_step(group, carry):
        low = high = jnp.zeros((8, FH), F32)
        for k in range(8):
            d = group * 8 + k
            here, total = fin_sum(group, k, fin_v, fin_low1, fin_high1, fin_side1, core)
            rhs = here + source_v[d]
            new = (rhs + total) * SEVENTH
            first[d + 1] = new
            base[d] = (OMEGA * SEVENTH) * rhs + (1.0 - OMEGA) * here
            low, high = pick_rows(k, new, low, high)
            pick_side(d, new, out_fin_side2, core)
        out_fin_low2[group] = low
        out_fin_high2[group] = high
        return carry

    lax.fori_loop(1, FD // 8, fin_step, 0)

    arrived(one, FIN_ABOVE)

    @pl.when(on_wall)
    def _():
        cells = (ROWS, CY)
        least = (2 * FH * iota(cells, 0) + 2 * iota(cells, 1)).astype(F32)
        roots = fin_v[1]
        surface = []
        for di in range(2):
            for dj in range(2):
                columns = dot(roots, spread(FH, CY, dj, 0))
                surface.append(dot(spread(ROWS, FW, di, 1), columns))
        shifts = (0.0, 1.0, float(FH), float(FH + 1))

        def owned(k, sums):
            offset = wall_in[k, ROWS:] - least
            temps = wall_in[k, :ROWS]
            value = jnp.zeros(cells, F32)
            new = []
            for part, shift, total in zip(surface, shifts, sums):
                hit = offset == shift
                value = jnp.where(hit, part, value)
                new.append(total + jnp.where(hit, temps - part, 0.0))
            back_out[k] = value
            return tuple(new)

        def step(k, sums):
            wall_link(k).wait_recv()
            sums = owned(k, sums)
            back_link(k).start()
            return sums

        sums = owned(0, (jnp.zeros(cells, F32),) * 4)
        sums = lax.fori_loop(1, blocks, step, sums)
        deposit = jnp.zeros((FW, FH), F32)
        for di in range(2):
            rows = spread(FW, ROWS, di, 0)
            for dj in range(2):
                deposit = deposit + dot(
                    dot(rows, sums[2 * di + dj]), spread(CY, FH, dj, 1)
                )
        fin_v[0] = deposit
        first[0] = deposit

    fin_step(0, 0)

    @pl.when(on_wall)
    def _():
        def step(k, total):
            back_link(k).wait_recv()
            return total + back_in[k]

        ghost = lax.fori_loop(1, blocks, step, back_out[0])
        square = jnp.concatenate([ghost, jnp.zeros((CY - ROWS, CY), F32)], axis=0)
        low2[...] = jnp.transpose(square)

        def fix(x, carry):
            lane = iota((CY, 128), 1)
            on = jnp.where(parity_rows((CY, 128)) == x % 2, active_v[x, :, :128], 0) == 1
            share = pltpu.roll(low2[...], (128 - x) % 128, 1) * SEVENTH
            half = red[x + 1, :, :128]
            red[x + 1, :, :128] = half + jnp.where(on & (lane == 0), share, 0.0)
            return carry

        lax.fori_loop(0, CX, fix, 0)

    start(two, FLUID_UP, FLUID_DOWN, FLUID_SIDE, FLUID_ABOVE, FLUID_BELOW,
          FIN_UP, FIN_DOWN, FIN_SIDE, FIN_ABOVE, FIN_BELOW)

    sent(one)

    @pl.when(on_wall)
    def _():
        def step(k, carry):
            wall_link(k).wait_send()
            back_link(k).wait_send()
            return carry

        lax.fori_loop(1, blocks, step, 0)

    arrived(two, *range(FACES))
    sent(two)


def second_kernel(
    red, active, first, base, side, low, high, fin_low, fin_high, fin_side,
    fluid_out, fin_out, fluid_v, fin_v, fluid_sem, fin_sem,
):
    core = lax.axis_index("gy")

    def fluid_copy(x):
        return pltpu.make_async_copy(fluid_v.at[x], fluid_out.at[x], fluid_sem.at[x])

    def fin_copy(group):
        part = pl.ds(group * 8, 8)
        return pltpu.make_async_copy(fin_v.at[part], fin_out.at[part], fin_sem.at[group])

    def black_step(x, carry):
        fluid_v[x] = fluid_plane(x, red, active, side, low, high, 1, core)
        fluid_copy(x).start()
        return carry

    lax.fori_loop(0, CX, black_step, 0)

    def fin_step(group, carry):
        for k in range(8):
            d = group * 8 + k
            _, total = fin_sum(group, k, first, fin_low, fin_high, fin_side, core)
            fin_v[d] = base[d] + (OMEGA * SEVENTH) * total
        fin_copy(group).start()
        return carry

    lax.fori_loop(0, FD // 8, fin_step, 0)

    def fluid_done(x, carry):
        fluid_copy(x).wait()
        return carry

    def fin_done(group, carry):
        fin_copy(group).wait()
        return carry

    lax.fori_loop(0, CX, fluid_done, 0)
    lax.fori_loop(0, FD // 8, fin_done, 0)


def local(sizes, fluid_temp, active, fin_temp, fin_source, wall_owner, wall_target):
    blocks = sizes[1]
    owner = wall_owner.reshape(CX, CY)
    target = wall_target.reshape(CX, CY)
    anywhere = pl.BlockSpec(memory_space=pl.ANY)
    vmem = pl.BlockSpec(memory_space=pltpu.VMEM)
    column, rows, strip = (CY, 128), (FD // 8, 8, FH), (FW, 128)
    shapes = [
        (CX + 2, CY, CZ), None, (FD + 2, FW, FH), (FD, FW, FH),
        (CX, 8, CZ), column, column, rows, rows, strip,
    ]
    held = [
        pltpu.VMEM((CX, CY, CZ), jnp.int32) if s is None else pltpu.VMEM(s, F32) for s in shapes
    ]
    dma = pltpu.SemaphoreType.DMA
    middle = pl.pallas_call(
        functools.partial(exchange_kernel, sizes),
        name="exchange_and_first_sweeps",
        out_shape=held,
        in_specs=[anywhere] * 6,
        out_specs=[vmem] * 10,
        scratch_shapes=[
            pltpu.VMEM((CX + 2, CY, CZ), F32),
            pltpu.VMEM((FD + 2, FW, FH), F32),
            pltpu.VMEM((FD, FW, FH), F32),
            pltpu.VMEM((CX, CY), jnp.int32),
            pltpu.VMEM((CX, CY), jnp.int32),
            pltpu.VMEM((CX, 8, CZ), F32),
            *[pltpu.VMEM(s, F32) for s in (column, column, rows, rows, strip)],
            *[pltpu.VMEM(s, F32) for s in (column, column, rows, rows, strip)],
            *[pltpu.VMEM(s, F32) for s in (column, column, rows, rows, strip)],
            pltpu.VMEM((blocks, 2 * ROWS, CY), F32),
            pltpu.VMEM((blocks, 2 * ROWS, CY), F32),
            pltpu.VMEM((blocks, ROWS, CY), F32),
            pltpu.VMEM((blocks, ROWS, CY), F32),
            dma((6,)),
            *[dma((FACES,)) for _ in range(4)],
            *[dma((blocks,)) for _ in range(4)],
        ],
        compiler_params=pltpu.CompilerParams(
            collective_id=0, has_side_effects=True, vmem_limit_bytes=40 * 2**20
        ),
    )(fluid_temp, active, fin_temp, fin_source, owner, target)
    return pl.pallas_call(
        second_kernel,
        name="second_sweeps",
        out_shape=[
            jax.ShapeDtypeStruct((CX, CY, CZ), F32),
            jax.ShapeDtypeStruct((FD, FW, FH), F32),
        ],
        in_specs=[vmem] * 10,
        out_specs=[anywhere] * 2,
        scratch_shapes=[
            pltpu.VMEM((CX, CY, CZ), F32),
            pltpu.VMEM((FD, FW, FH), F32),
            dma((CX,)),
            dma((FD // 8,)),
        ],
        compiler_params=pltpu.CompilerParams(vmem_limit_bytes=40 * 2**20),
    )(*middle)


def solution(mesh):
    in_specs = (
        P("gx", "gy", "grp"),
        P("gx", "gy", "grp"),
        P("grp", "gx", "gy"),
        P("grp", "gx", "gy"),
        P("gx", "gy", None, None),
        P("gx", "gy", None),
    )
    out_specs = (P("gx", "gy", "grp"), P("grp", "gx", "gy"))
    sizes = (mesh.shape["grp"], mesh.shape["gx"])
    body = functools.partial(local, sizes)
    return jax.shard_map(body, mesh=mesh, in_specs=in_specs, out_specs=out_specs, check_vma=False)
```

```python
import functools

import jax
import jax.numpy as jnp
from jax import lax
from jax.experimental import pallas as pl
from jax.experimental.pallas import tpu as pltpu
from jax.sharding import PartitionSpec as P

F32 = jnp.float32
MESH = pl.DeviceIdType.MESH
DIAG = 7.0
SPECTRAL = 6.0 / DIAG
OMEGA = 1.0 / (1.0 - SPECTRAL * SPECTRAL / 2.0)
SEVENTH = 1.0 / 7.0

CX, CY, CZ = 16, 128, 256
FD, FW, FH = 64, 32, 256
ROWS = CX

HALF = CY // 2

FLUID_UP, FLUID_DOWN, FLUID_SIDE = (0, 1), (2, 3), (4, 5)
FLUID_ABOVE, FLUID_BELOW = 6, 7
FIN_UP, FIN_DOWN, FIN_SIDE, FIN_ABOVE, FIN_BELOW = 8, 9, 10, 11, 12
FACES = 13


def iota(shape, axis):
    return lax.broadcasted_iota(jnp.int32, shape, axis)


def parity_rows(shape):
    rows, lanes = shape
    tile = (iota((8, lanes), 0) + iota((8, lanes), 1)) % 2
    return jnp.concatenate([tile] * (rows // 8), axis=0)


def shifted_rows(plane, low_tile, high_tile):
    rows, lanes = plane.shape
    sub = iota((8, lanes), 0)
    up = pltpu.roll(plane, 1, 0)
    down = pltpu.roll(plane, rows - 1, 0)
    up = jnp.concatenate([jnp.where(sub == 0, low_tile, up[:8]), up[8:]], axis=0)
    down = jnp.concatenate([down[:-8], jnp.where(sub == 7, high_tile, down[-8:])], axis=0)
    return up + down


def shifted_lanes(plane, low_tile, high_tile):
    rows, lanes = plane.shape
    lane = iota((rows, 128), 1)
    left = pltpu.roll(plane, 1, 1)
    right = pltpu.roll(plane, lanes - 1, 1)
    first = jnp.where(lane == 0, low_tile, left[:, :128]) + right[:, :128]
    last = left[:, 128:] + jnp.where(lane == 127, high_tile, right[:, 128:])
    return jnp.concatenate([first, last], axis=1)


def fluid_plane(x, field, active, side, low, high, parity, core):
    here = field[x + 1]
    total = field[x] + field[x + 2]
    tile = side[x]
    low_tile = jnp.where(core == 1, pltpu.roll(tile, 1, 0), 0.0)
    high_tile = jnp.where(core == 0, pltpu.roll(tile, 7, 0), 0.0)
    total = total + shifted_rows(here, low_tile, high_tile)
    low_lane = pltpu.roll(low[...], (128 - x) % 128, 1)
    high_lane = pltpu.roll(high[...], 127 - x, 1)
    total = total + shifted_lanes(here, low_lane, high_lane)
    on = jnp.where(parity_rows(here.shape) == (x + parity) % 2, active[x], 0) == 1
    return jnp.where(on, (here + total) * SEVENTH, here)


def fin_sum(group, k, field, low, high, side, core):
    d = group * 8 + k
    here = field[d + 1]
    total = field[d] + field[d + 2]
    low_tile = pltpu.roll(low[group], (8 - k) % 8, 0)
    high_tile = pltpu.roll(high[group], 7 - k, 0)
    total = total + shifted_rows(here, low_tile, high_tile)
    column = pltpu.roll(side[...], jnp.where(core == 1, (128 - d) % 128, 127 - d), 1)
    total = total + shifted_lanes(
        here, jnp.where(core == 1, column, 0.0), jnp.where(core == 0, column, 0.0)
    )
    return here, total


def pick_columns(x, plane, low, high):
    lane = iota((plane.shape[0], 128), 1)
    low[...] = jnp.where(lane == x, pltpu.roll(plane[:, :128], x, 1), low[...])
    high[...] = jnp.where(lane == x, pltpu.roll(plane[:, 128:], (x + 1) % 128, 1), high[...])


def one_colour(plane, colour):
    folded = pltpu.roll(plane[HALF:], HALF - 1, 0)
    return jnp.where(parity_rows(folded.shape) == colour, plane[:HALF], folded)


def both_halves(folded):
    return jnp.concatenate([folded, pltpu.roll(folded, 1, 0)], axis=0)


def as_rows(columns):
    return jnp.transpose(columns)[:ROWS]


def as_columns(rows):
    square = jnp.concatenate([rows, jnp.zeros((CY - ROWS, CY), F32)], axis=0)
    return jnp.transpose(square)


def pick_rows(k, plane, low, high):
    sub = iota((8, plane.shape[1]), 0)
    low = jnp.where(sub == k, pltpu.roll(plane[:8], k, 0), low)
    high = jnp.where(sub == k, pltpu.roll(plane[-8:], (k + 1) % 8, 0), high)
    return low, high


def pick_side(d, plane, out, core):
    lane = iota((plane.shape[0], 128), 1)
    half = jnp.where(core == 0, plane[:, 128:], plane[:, :128])
    turned = pltpu.roll(half, jnp.where(core == 0, (d + 1) % 128, d), 1)
    out[...] = jnp.where(lane == d, turned, out[...])


def spread(rows, columns, offset, axis):
    a, b = iota((rows, columns), axis), iota((rows, columns), 1 - axis)
    return jnp.where(a == 2 * b + offset, 1.0, 0.0).astype(F32)


def dot(a, b):
    return jnp.dot(a, b, precision=lax.Precision.HIGHEST, preferred_element_type=F32)


def exchange_kernel(
    sizes,
    fluid, active, fin, source, owner, target,
    red, active_v, first, base, side2, low2, high2, fin_low2, fin_high2, fin_side2,
    fluid_v, fin_v, source_v, owner_v, target_v,
    side1, low1, high1, fin_low1, fin_high1, fin_side1,
    out_fin_low1, out_fin_high1, out_fin_side1, out_fin_low2, out_fin_high2, out_fin_side2,
    low_column, high_column,
    out_low1, out_high1, in_low1, in_high1, out_low2, out_high2, in_low2, in_high2,
    out_up1, out_down1, in_up1, in_down1, out_up2, out_down2, in_up2, in_down2,
    wall_out, wall_in, back_out, back_in,
    load_sem, send1, recv1, send2, recv2, wall_send, wall_recv, back_send, back_recv,
):
    groups, blocks = sizes
    grp, gx, core = lax.axis_index("grp"), lax.axis_index("gx"), lax.axis_index("gy")
    has_low, has_high = gx > 0, gx < blocks - 1
    has_below, has_above = grp > 0, grp < groups - 1
    on_wall = grp == 0
    left, right = (grp, gx - 1, core), (grp, gx + 1, core)
    below, above = (grp - 1, gx, core), (grp + 1, gx, core)
    other = (grp, gx, 1 - core)

    def peer(k):
        return (grp, lax.rem(gx + k, blocks), core)

    def peer_back(k):
        return (grp, lax.rem(gx - k + blocks, blocks), core)

    loads = [
        pltpu.make_async_copy(owner, owner_v, load_sem.at[0]),
        pltpu.make_async_copy(target, target_v, load_sem.at[1]),
        pltpu.make_async_copy(fluid, fluid_v.at[pl.ds(1, CX)], load_sem.at[2]),
        pltpu.make_async_copy(fin, fin_v.at[pl.ds(1, FD)], load_sem.at[3]),
        pltpu.make_async_copy(active, active_v, load_sem.at[4]),
        pltpu.make_async_copy(source, source_v, load_sem.at[5]),
    ]
    for load in loads:
        load.start()

    barrier = pltpu.get_barrier_semaphore()

    def greet(device):
        pl.semaphore_signal(barrier, inc=1, device_id=device, device_id_type=MESH)

    greet(other)

    @pl.when(has_above)
    def _():
        greet(above)

    @pl.when(has_below)
    def _():
        greet(below)

    @pl.when(on_wall)
    def _():
        def step(k, carry):
            greet(peer(k))
            return carry

        lax.fori_loop(1, blocks, step, 0)

    @pl.when(jnp.logical_not(on_wall) & has_low)
    def _():
        greet(left)

    @pl.when(jnp.logical_not(on_wall) & has_high)
    def _():
        greet(right)

    @pl.when(jnp.logical_not(has_low))
    def _():
        fluid_v[0] = jnp.zeros((CY, CZ), F32)
        red[0] = jnp.zeros((CY, CZ), F32)
        fin_low1[...] = jnp.zeros(fin_low1.shape, F32)
        fin_low2[...] = jnp.zeros(fin_low2.shape, F32)

    @pl.when(jnp.logical_not(has_high))
    def _():
        fluid_v[CX + 1] = jnp.zeros((CY, CZ), F32)
        red[CX + 1] = jnp.zeros((CY, CZ), F32)
        fin_high1[...] = jnp.zeros(fin_high1.shape, F32)
        fin_high2[...] = jnp.zeros(fin_high2.shape, F32)

    @pl.when(jnp.logical_not(has_below))
    def _():
        in_low1[...] = jnp.zeros(in_low1.shape, F32)

    @pl.when(jnp.logical_not(has_above))
    def _():
        in_high1[...] = jnp.zeros(in_high1.shape, F32)
        in_high2[...] = jnp.zeros(in_high2.shape, F32)
        fin_v[FD + 1] = jnp.zeros((FW, FH), F32)
        first[FD + 1] = jnp.zeros((FW, FH), F32)

    for ref in (low_column, high_column, out_fin_side1, out_fin_side2):
        ref[...] = jnp.zeros(ref.shape, F32)

    loads[0].wait()
    loads[1].wait()
    loads[2].wait()

    def pack_fluid(x, carry):
        pick_columns(x, fluid_v[x + 1], low_column, high_column)
        return carry

    lax.fori_loop(0, CX, pack_fluid, 0)
    out_low1[...] = as_rows(low_column[...])
    out_high1[...] = as_rows(high_column[...])

    def fold(field, x, colour, out, half):
        out[half] = one_colour(field[x + 1, :, half * 128 : half * 128 + 128], colour)

    for half in range(2):
        fold(fluid_v, CX - 1, 0, out_up1, half)
        fold(fluid_v, 0, 1, out_down1, half)

    expected = 1 + has_above.astype(jnp.int32) + has_below.astype(jnp.int32)
    sides = has_low.astype(jnp.int32) + has_high.astype(jnp.int32)
    pl.semaphore_wait(barrier, expected + jnp.where(on_wall, blocks - 1, sides))

    def link(src, dst, send, recv, k, device):
        return pltpu.make_async_remote_copy(
            src_ref=src, dst_ref=dst, send_sem=send.at[k], recv_sem=recv.at[k],
            device_id=device, device_id_type=MESH,
        )

    def wall_link(k):
        return link(wall_out.at[k], wall_in.at[k], wall_send, wall_recv, k, peer(k))

    def back_link(k):
        return link(back_out.at[k], back_in.at[k], back_send, back_recv, k, peer_back(k))

    @pl.when(on_wall)
    def _():
        temps = out_low1[...]
        owners = owner_v[...]
        targets = target_v[...].astype(F32)

        def masked(k, out):
            out[k, :ROWS] = temps
            out[k, ROWS:] = jnp.where(owners == lax.rem(gx + k, blocks), targets, -1.0)

        def step(k, carry):
            masked(k, wall_out)
            wall_link(k).start()
            return carry

        masked(0, wall_in)
        lax.fori_loop(1, blocks, step, 0)

    side_row = pl.multiple_of(jnp.where(core == 0, CY - 8, 0), 8)

    def faces(send, recv, side_from, out_up, in_up, out_down, in_down, side, out_low, in_low, out_high, in_high,
              fin_from, fin_to, fin_low, fin_high, fin_side, sent_fin_low, sent_fin_high, sent_fin_side):
        links = {
            FLUID_ABOVE: (link(out_high, in_low, send, recv, FLUID_ABOVE, above), has_above, has_below),
            FLUID_BELOW: (link(out_low, in_high, send, recv, FLUID_BELOW, below), has_below, has_above),
            FIN_UP: (link(sent_fin_high, fin_low, send, recv, FIN_UP, right), has_high, has_low),
            FIN_DOWN: (link(sent_fin_low, fin_high, send, recv, FIN_DOWN, left), has_low, has_high),
            FIN_SIDE: (link(sent_fin_side, fin_side, send, recv, FIN_SIDE, other), None, None),
            FIN_ABOVE: (link(fin_from.at[FD], fin_to.at[0], send, recv, FIN_ABOVE, above), has_above, has_below),
            FIN_BELOW: (link(fin_from.at[1], fin_to.at[FD + 1], send, recv, FIN_BELOW, below), has_below, has_above),
        }
        for half in range(2):
            up, down, across = FLUID_UP[half], FLUID_DOWN[half], FLUID_SIDE[half]
            lanes = pl.ds(half * 128, 128)
            rim = side_from.at[pl.ds(1, CX), pl.ds(side_row, 8), lanes]
            links[up] = (link(out_up.at[half], in_up.at[half], send, recv, up, right), has_high, has_low)
            links[down] = (link(out_down.at[half], in_down.at[half], send, recv, down, left), has_low, has_high)
            links[across] = (link(rim, side.at[:, :, lanes], send, recv, across, other), None, None)
        return links

    def when(condition, action):
        if condition is None:
            action()
        else:
            pl.when(condition)(action)

    one = faces(send1, recv1, fluid_v, out_up1, in_up1, out_down1, in_down1, side1, out_low1, in_low1, out_high1, in_high1,
                fin_v, fin_v, fin_low1, fin_high1, fin_side1, out_fin_low1, out_fin_high1, out_fin_side1)
    two = faces(send2, recv2, red, out_up2, in_up2, out_down2, in_down2, side2, out_low2, in_low2, out_high2, in_high2,
                first, first, fin_low2, fin_high2, fin_side2, out_fin_low2, out_fin_high2, out_fin_side2)

    def start(links, *which):
        for k in which:
            when(links[k][1], links[k][0].start)

    def arrived(links, *which):
        for k in which:
            when(links[k][2], links[k][0].wait_recv)

    def sent(links):
        for k in range(FACES):
            when(links[k][1], links[k][0].wait_send)

    start(one, *FLUID_UP, *FLUID_DOWN, *FLUID_SIDE, FLUID_ABOVE, FLUID_BELOW)

    loads[3].wait()
    start(one, FIN_ABOVE, FIN_BELOW)

    def pack_fin(group, carry):
        low = high = jnp.zeros((8, FH), F32)
        for k in range(8):
            plane = fin_v[group * 8 + k + 1]
            low, high = pick_rows(k, plane, low, high)
            pick_side(group * 8 + k, plane, out_fin_side1, core)
        out_fin_low1[group] = low
        out_fin_high1[group] = high
        return carry

    lax.fori_loop(0, FD // 8, pack_fin, 0)
    start(one, FIN_SIDE, FIN_UP, FIN_DOWN)

    loads[4].wait()
    loads[5].wait()
    arrived(one, *FLUID_SIDE, FLUID_ABOVE, FLUID_BELOW)
    low1[...] = as_columns(in_low1[...])
    high1[...] = as_columns(in_high1[...])

    def red_step(x, carry):
        new = fluid_plane(x, fluid_v, active_v, side1, low1, high1, 0, core)
        red[x + 1] = new
        pick_columns(x, new, low_column, high_column)
        return carry

    lax.fori_loop(1, CX - 1, red_step, 0)

    @pl.when(on_wall)
    def _():
        cells = (ROWS, CY)
        least = (2 * FH * iota(cells, 0) + 2 * iota(cells, 1)).astype(F32)
        roots = fin_v[1]
        surface = []
        for di in range(2):
            for dj in range(2):
                columns = dot(roots, spread(FH, CY, dj, 0))
                surface.append(dot(spread(ROWS, FW, di, 1), columns))
        shifts = (0.0, 1.0, float(FH), float(FH + 1))

        def owned(k, sums):
            offset = wall_in[k, ROWS:] - least
            temps = wall_in[k, :ROWS]
            value = jnp.zeros(cells, F32)
            new = []
            for part, shift, total in zip(surface, shifts, sums):
                hit = offset == shift
                value = jnp.where(hit, part, value)
                new.append(total + jnp.where(hit, temps - part, 0.0))
            back_out[k] = value
            return tuple(new)

        def step(k, sums):
            wall_link(k).wait_recv()
            sums = owned(k, sums)
            back_link(k).start()
            return sums

        sums = owned(0, (jnp.zeros(cells, F32),) * 4)
        sums = lax.fori_loop(1, blocks, step, sums)
        deposit = jnp.zeros((FW, FH), F32)
        for di in range(2):
            rows = spread(FW, ROWS, di, 0)
            for dj in range(2):
                deposit = deposit + dot(
                    dot(rows, sums[2 * di + dj]), spread(CY, FH, dj, 1)
                )
        fin_v[0] = deposit
        first[0] = deposit

    def unfold(arrived_up, arrived_down, field):
        def low_plane():
            for half in range(2):
                field[0, :, half * 128 : half * 128 + 128] = both_halves(arrived_up[half])

        def high_plane():
            for half in range(2):
                field[CX + 1, :, half * 128 : half * 128 + 128] = both_halves(arrived_down[half])

        when(has_low, low_plane)
        when(has_high, high_plane)

    arrived(one, *FLUID_UP, *FLUID_DOWN)
    unfold(in_up1, in_down1, fluid_v)
    red_step(0, 0)
    red_step(CX - 1, 0)
    out_low2[...] = as_rows(low_column[...])
    out_high2[...] = as_rows(high_column[...])
    fold(red, CX - 1, 1, out_up2, 1)
    fold(red, 0, 0, out_down2, 1)
    start(two, FLUID_UP[1], FLUID_DOWN[1], FLUID_SIDE[1], FLUID_ABOVE, FLUID_BELOW)

    arrived(one, FIN_SIDE, FIN_UP, FIN_DOWN, FIN_BELOW, FIN_ABOVE)

    def fin_step(group, carry):
        low = high = jnp.zeros((8, FH), F32)
        for k in range(8):
            d = group * 8 + k
            here, total = fin_sum(group, k, fin_v, fin_low1, fin_high1, fin_side1, core)
            rhs = here + source_v[d]
            new = (rhs + total) * SEVENTH
            first[d + 1] = new
            base[d] = (OMEGA * SEVENTH) * rhs + (1.0 - OMEGA) * here
            low, high = pick_rows(k, new, low, high)
            pick_side(d, new, out_fin_side2, core)
        out_fin_low2[group] = low
        out_fin_high2[group] = high
        return carry

    lax.fori_loop(0, FD // 8, fin_step, 0)
    start(two, FIN_UP, FIN_DOWN, FIN_SIDE, FIN_ABOVE, FIN_BELOW)

    @pl.when(on_wall)
    def _():
        def step(k, total):
            back_link(k).wait_recv()
            return total + back_in[k]

        ghost = lax.fori_loop(1, blocks, step, back_out[0])
        in_low2[...] = ghost
        low2[...] = as_columns(ghost)

        def fix(x, carry):
            lane = iota((CY, 128), 1)
            on = jnp.where(parity_rows((CY, 128)) == x % 2, active_v[x, :, :128], 0) == 1
            share = pltpu.roll(low2[...], (128 - x) % 128, 1) * SEVENTH
            half = red[x + 1, :, :128]
            red[x + 1, :, :128] = half + jnp.where(on & (lane == 0), share, 0.0)
            return carry

        lax.fori_loop(0, CX, fix, 0)

    fold(red, CX - 1, 1, out_up2, 0)
    fold(red, 0, 0, out_down2, 0)
    start(two, FLUID_UP[0], FLUID_DOWN[0], FLUID_SIDE[0])

    sent(one)

    @pl.when(on_wall)
    def _():
        def step(k, carry):
            wall_link(k).wait_send()
            back_link(k).wait_send()
            return carry

        lax.fori_loop(1, blocks, step, 0)

    arrived(two, *range(FACES))
    low2[...] = as_columns(in_low2[...])
    high2[...] = as_columns(in_high2[...])
    unfold(in_up2, in_down2, red)
    sent(two)


def second_kernel(
    red, active, first, base, side, low, high, fin_low, fin_high, fin_side,
    fluid_out, fin_out, fluid_v, fin_v, fluid_sem, fin_sem,
):
    core = lax.axis_index("gy")

    def fluid_copy(x):
        return pltpu.make_async_copy(fluid_v.at[x], fluid_out.at[x], fluid_sem.at[x])

    def fin_copy(group):
        part = pl.ds(group * 8, 8)
        return pltpu.make_async_copy(fin_v.at[part], fin_out.at[part], fin_sem.at[group])

    def black_step(x, carry):
        fluid_v[x] = fluid_plane(x, red, active, side, low, high, 1, core)
        fluid_copy(x).start()
        return carry

    lax.fori_loop(0, CX, black_step, 0)

    def fin_step(group, carry):
        for k in range(8):
            d = group * 8 + k
            _, total = fin_sum(group, k, first, fin_low, fin_high, fin_side, core)
            fin_v[d] = base[d] + (OMEGA * SEVENTH) * total
        fin_copy(group).start()
        return carry

    lax.fori_loop(0, FD // 8, fin_step, 0)

    def fluid_done(x, carry):
        fluid_copy(x).wait()
        return carry

    def fin_done(group, carry):
        fin_copy(group).wait()
        return carry

    lax.fori_loop(0, CX, fluid_done, 0)
    lax.fori_loop(0, FD // 8, fin_done, 0)


def local(sizes, fluid_temp, active, fin_temp, fin_source, wall_owner, wall_target):
    blocks = sizes[1]
    owner = wall_owner.reshape(CX, CY)
    target = wall_target.reshape(CX, CY)
    anywhere = pl.BlockSpec(memory_space=pl.ANY)
    vmem = pl.BlockSpec(memory_space=pltpu.VMEM)
    column, rows, strip = (CY, 128), (FD // 8, 8, FH), (FW, 128)
    shapes = [
        (CX + 2, CY, CZ), None, (FD + 2, FW, FH), (FD, FW, FH),
        (CX, 8, CZ), column, column, rows, rows, strip,
    ]
    held = [
        pltpu.VMEM((CX, CY, CZ), jnp.int32) if s is None else pltpu.VMEM(s, F32) for s in shapes
    ]
    dma = pltpu.SemaphoreType.DMA
    in_hbm = [
        pltpu.with_memory_space_constraint(x, pltpu.HBM)
        for x in (fluid_temp, active, fin_temp, fin_source)
    ]
    middle = pl.pallas_call(
        functools.partial(exchange_kernel, sizes),
        name="exchange_and_first_sweeps",
        out_shape=held,
        in_specs=[anywhere] * 6,
        out_specs=[vmem] * 10,
        scratch_shapes=[
            pltpu.VMEM((CX + 2, CY, CZ), F32),
            pltpu.VMEM((FD + 2, FW, FH), F32),
            pltpu.VMEM((FD, FW, FH), F32),
            pltpu.VMEM((CX, CY), jnp.int32),
            pltpu.VMEM((CX, CY), jnp.int32),
            pltpu.VMEM((CX, 8, CZ), F32),
            *[pltpu.VMEM(s, F32) for s in (column, column, rows, rows, strip)],
            *[pltpu.VMEM(s, F32) for s in (rows, rows, strip)],
            *[pltpu.VMEM(s, F32) for s in (rows, rows, strip)],
            *[pltpu.VMEM(column, F32) for _ in range(2)],
            *[pltpu.VMEM((ROWS, CY), F32) for _ in range(8)],
            *[pltpu.VMEM((2, HALF, 128), F32) for _ in range(8)],
            pltpu.VMEM((blocks, 2 * ROWS, CY), F32),
            pltpu.VMEM((blocks, 2 * ROWS, CY), F32),
            pltpu.VMEM((blocks, ROWS, CY), F32),
            pltpu.VMEM((blocks, ROWS, CY), F32),
            dma((6,)),
            *[dma((FACES,)) for _ in range(4)],
            *[dma((blocks,)) for _ in range(4)],
        ],
        compiler_params=pltpu.CompilerParams(
            collective_id=0, has_side_effects=True, vmem_limit_bytes=40 * 2**20
        ),
    )(*in_hbm, owner, target)
    return pl.pallas_call(
        second_kernel,
        name="second_sweeps",
        out_shape=[
            jax.ShapeDtypeStruct((CX, CY, CZ), F32),
            jax.ShapeDtypeStruct((FD, FW, FH), F32),
        ],
        in_specs=[vmem] * 10,
        out_specs=[anywhere] * 2,
        scratch_shapes=[
            pltpu.VMEM((CX, CY, CZ), F32),
            pltpu.VMEM((FD, FW, FH), F32),
            dma((CX,)),
            dma((FD // 8,)),
        ],
        compiler_params=pltpu.CompilerParams(vmem_limit_bytes=40 * 2**20),
    )(*middle)


def solution(mesh):
    in_specs = (
        P("gx", "gy", "grp"),
        P("gx", "gy", "grp"),
        P("grp", "gx", "gy"),
        P("grp", "gx", "gy"),
        P("gx", "gy", None, None),
        P("gx", "gy", None),
    )
    out_specs = (P("gx", "gy", "grp"), P("grp", "gx", "gy"))
    sizes = (mesh.shape["grp"], mesh.shape["gx"])
    body = functools.partial(local, sizes)
    return jax.shard_map(body, mesh=mesh, in_specs=in_specs, out_specs=out_specs, check_vma=False)
```

```python
import functools

import jax
import jax.numpy as jnp
from jax import lax
from jax.experimental import pallas as pl
from jax.experimental.pallas import tpu as pltpu
from jax.sharding import PartitionSpec as P

F32 = jnp.float32
MESH = pl.DeviceIdType.MESH
DIAG = 7.0
SPECTRAL = 6.0 / DIAG
OMEGA = 1.0 / (1.0 - SPECTRAL * SPECTRAL / 2.0)
SEVENTH = 1.0 / 7.0

CX, CY, CZ = 16, 128, 256
FD, FW, FH = 64, 32, 256
ROWS = CX

HALF = CY // 2
PAIRS = CX // 2
CHUNK = 32

FLUID_UP, FLUID_DOWN, FLUID_SIDE = (0, 1), (2, 3), (4, 5)
FLUID_ABOVE, FLUID_BELOW = 6, 7
FIN_UP, FIN_DOWN, FIN_SIDE, FIN_ABOVE, FIN_BELOW = 8, 9, 10, 11, 12
FACES = 13


def iota(shape, axis):
    return lax.broadcasted_iota(jnp.int32, shape, axis)


def parity_rows(shape):
    rows, lanes = shape
    tile = (iota((8, lanes), 0) + iota((8, lanes), 1)) % 2
    return jnp.concatenate([tile] * (rows // 8), axis=0)


def shifted_rows(plane, low_tile, high_tile):
    rows, lanes = plane.shape
    sub = iota((8, lanes), 0)
    up = pltpu.roll(plane, 1, 0)
    down = pltpu.roll(plane, rows - 1, 0)
    up = jnp.concatenate([jnp.where(sub == 0, low_tile, up[:8]), up[8:]], axis=0)
    down = jnp.concatenate([down[:-8], jnp.where(sub == 7, high_tile, down[-8:])], axis=0)
    return up + down


def shifted_lanes(plane, low_tile, high_tile):
    rows, lanes = plane.shape
    lane = iota((rows, 128), 1)
    left = pltpu.roll(plane, 1, 1)
    right = pltpu.roll(plane, lanes - 1, 1)
    first = jnp.where(lane == 0, low_tile, left[:, :128]) + right[:, :128]
    last = left[:, 128:] + jnp.where(lane == 127, high_tile, right[:, 128:])
    return jnp.concatenate([first, last], axis=1)


def half_sweep(pair, source, target, active, side, low, high, red, core, put):
    x = 2 * pair
    for start in range(0, CY, CHUNK):
        rows = slice(start, start + CHUNK)
        even = parity_rows((CHUNK, CZ)) == 0
        here = source[pair + 1, rows]
        before, after = source[pair, rows], source[pair + 2, rows]
        near, far = active[x, rows], active[x + 1, rows]
        if red:
            total = here + jnp.where(even, before, after)
            on = jnp.where(even, near, far) == 1
        else:
            total = here + jnp.where(even, after, before)
            on = jnp.where(even, far, near) == 1
        if start == 0:
            low_tile = jnp.where(core == 1, pltpu.roll(side[pair], 1, 0), 0.0)
        else:
            low_tile = pltpu.roll(source[pair + 1, start - 8 : start], 1, 0)
        stop = start + CHUNK
        if stop == CY:
            high_tile = jnp.where(core == 0, pltpu.roll(side[pair], 7, 0), 0.0)
        else:
            high_tile = pltpu.roll(source[pair + 1, stop : stop + 8], 7, 0)
        total = total + shifted_rows(here, low_tile, high_tile)
        low_lane = pltpu.roll(low[rows], (128 - x) % 128, 1)
        high_lane = pltpu.roll(high[rows], 127 - x, 1)
        total = total + shifted_lanes(here, low_lane, high_lane)
        old = target[pair + 1, rows]
        put(rows, here, jnp.where(on, (old + total) * SEVENTH, old))


def fin_sum(group, k, field, low, high, side, core):
    d = group * 8 + k
    here = field[d + 1]
    total = field[d] + field[d + 2]
    low_tile = pltpu.roll(low[group], (8 - k) % 8, 0)
    high_tile = pltpu.roll(high[group], 7 - k, 0)
    total = total + shifted_rows(here, low_tile, high_tile)
    column = pltpu.roll(side[...], jnp.where(core == 1, (128 - d) % 128, 127 - d), 1)
    total = total + shifted_lanes(
        here, jnp.where(core == 1, column, 0.0), jnp.where(core == 0, column, 0.0)
    )
    return here, total


def pick_low(x, plane, low, rows=slice(None)):
    lane = iota((plane.shape[0], 128), 1)
    low[rows] = jnp.where(lane == x, pltpu.roll(plane[:, :128], x, 1), low[rows])


def pick_high(x, plane, high, rows=slice(None)):
    lane = iota((plane.shape[0], 128), 1)
    high[rows] = jnp.where(lane == x, pltpu.roll(plane[:, 128:], (x + 1) % 128, 1), high[rows])


def one_colour(plane, colour):
    folded = pltpu.roll(plane[HALF:], HALF - 1, 0)
    return jnp.where(parity_rows(folded.shape) == colour, plane[:HALF], folded)


def both_halves(folded):
    return jnp.concatenate([folded, pltpu.roll(folded, 1, 0)], axis=0)


def as_rows(columns):
    return jnp.transpose(columns)[:ROWS]


def as_columns(rows):
    square = jnp.concatenate([rows, jnp.zeros((CY - ROWS, CY), F32)], axis=0)
    return jnp.transpose(square)


def pick_rows(k, plane, low, high):
    sub = iota((8, plane.shape[1]), 0)
    low = jnp.where(sub == k, pltpu.roll(plane[:8], k, 0), low)
    high = jnp.where(sub == k, pltpu.roll(plane[-8:], (k + 1) % 8, 0), high)
    return low, high


def pick_side(d, plane, out, core):
    lane = iota((plane.shape[0], 128), 1)
    half = jnp.where(core == 0, plane[:, 128:], plane[:, :128])
    turned = pltpu.roll(half, jnp.where(core == 0, (d + 1) % 128, d), 1)
    out[...] = jnp.where(lane == d, turned, out[...])


def spread(rows, columns, offset, axis):
    a, b = iota((rows, columns), axis), iota((rows, columns), 1 - axis)
    return jnp.where(a == 2 * b + offset, 1.0, 0.0).astype(F32)


def dot(a, b):
    return jnp.dot(a, b, precision=lax.Precision.HIGHEST, preferred_element_type=F32)


def exchange_kernel(
    sizes,
    fluid, active, fin, source, owner, target,
    red, black, active_v, base, side2, low2, high2,
    fluid_v, fin_v, first, source_v, owner_v, target_v,
    side1, low1, high1, fin_low1, fin_high1, fin_side1, fin_low2, fin_high2, fin_side2,
    out_fin_low1, out_fin_high1, out_fin_side1, out_fin_low2, out_fin_high2, out_fin_side2,
    low_column, high_column,
    out_low1, out_high1, in_low1, in_high1, out_low2, out_high2, in_low2, in_high2,
    out_up1, out_down1, in_up1, in_down1, out_up2, out_down2, in_up2, in_down2,
    wall_out, wall_in, back_out, back_in,
    load_sem, send1, recv1, send2, recv2, wall_send, wall_recv, back_send, back_recv,
):
    groups, blocks = sizes
    grp, gx, core = lax.axis_index("grp"), lax.axis_index("gx"), lax.axis_index("gy")
    has_low, has_high = gx > 0, gx < blocks - 1
    has_below, has_above = grp > 0, grp < groups - 1
    on_wall = grp == 0
    left, right = (grp, gx - 1, core), (grp, gx + 1, core)
    below, above = (grp - 1, gx, core), (grp + 1, gx, core)
    other = (grp, gx, 1 - core)

    def peer(k):
        return (grp, lax.rem(gx + k, blocks), core)

    def peer_back(k):
        return (grp, lax.rem(gx - k + blocks, blocks), core)

    loads = [
        pltpu.make_async_copy(owner, owner_v, load_sem.at[0]),
        pltpu.make_async_copy(target, target_v, load_sem.at[1]),
        pltpu.make_async_copy(fluid, fluid_v, load_sem.at[2]),
        pltpu.make_async_copy(fin, fin_v.at[pl.ds(1, FD)], load_sem.at[3]),
        pltpu.make_async_copy(active, active_v, load_sem.at[4]),
        pltpu.make_async_copy(source, source_v, load_sem.at[5]),
    ]
    for load in loads:
        load.start()

    barrier = pltpu.get_barrier_semaphore()

    def greet(device):
        pl.semaphore_signal(barrier, inc=1, device_id=device, device_id_type=MESH)

    greet(other)

    @pl.when(has_above)
    def _():
        greet(above)

    @pl.when(has_below)
    def _():
        greet(below)

    @pl.when(on_wall)
    def _():
        def step(k, carry):
            greet(peer(k))
            return carry

        lax.fori_loop(1, blocks, step, 0)

    @pl.when(jnp.logical_not(on_wall) & has_low)
    def _():
        greet(left)

    @pl.when(jnp.logical_not(on_wall) & has_high)
    def _():
        greet(right)

    @pl.when(jnp.logical_not(has_low))
    def _():
        black[0] = jnp.zeros((CY, CZ), F32)
        red[0] = jnp.zeros((CY, CZ), F32)
        fin_low1[...] = jnp.zeros(fin_low1.shape, F32)
        fin_low2[...] = jnp.zeros(fin_low2.shape, F32)

    @pl.when(jnp.logical_not(has_high))
    def _():
        black[PAIRS + 1] = jnp.zeros((CY, CZ), F32)
        red[PAIRS + 1] = jnp.zeros((CY, CZ), F32)
        fin_high1[...] = jnp.zeros(fin_high1.shape, F32)
        fin_high2[...] = jnp.zeros(fin_high2.shape, F32)

    @pl.when(jnp.logical_not(has_below))
    def _():
        in_low1[...] = jnp.zeros(in_low1.shape, F32)

    @pl.when(jnp.logical_not(has_above))
    def _():
        in_high1[...] = jnp.zeros(in_high1.shape, F32)
        in_high2[...] = jnp.zeros(in_high2.shape, F32)
        fin_v[FD + 1] = jnp.zeros((FW, FH), F32)
        first[FD + 1] = jnp.zeros((FW, FH), F32)

    for ref in (low_column, high_column, out_fin_side1, out_fin_side2):
        ref[...] = jnp.zeros(ref.shape, F32)

    loads[2].wait()

    def pack_fluid(pair, carry):
        x = 2 * pair
        for start in range(0, CY, CHUNK):
            rows = slice(start, start + CHUNK)
            even = parity_rows((CHUNK, CZ)) == 0
            near, far = fluid_v[x, rows], fluid_v[x + 1, rows]
            reds, blacks = jnp.where(even, near, far), jnp.where(even, far, near)
            red[pair + 1, rows] = reds
            black[pair + 1, rows] = blacks
            pick_low(x, blacks, low_column, rows)
            pick_low(x + 1, reds, low_column, rows)
            pick_high(x, blacks, high_column, rows)
        return carry

    lax.fori_loop(0, PAIRS, pack_fluid, 0)
    out_low1[...] = as_rows(low_column[...])
    out_high1[...] = as_rows(high_column[...])

    def fold(field, pair, colour, out, half):
        out[half] = one_colour(field[pair + 1, :, half * 128 : half * 128 + 128], colour)

    for half in range(2):
        fold(black, PAIRS - 1, 0, out_up1, half)
        fold(black, 0, 1, out_down1, half)

    loads[0].wait()
    loads[1].wait()

    expected = 1 + has_above.astype(jnp.int32) + has_below.astype(jnp.int32)
    sides = has_low.astype(jnp.int32) + has_high.astype(jnp.int32)
    pl.semaphore_wait(barrier, expected + jnp.where(on_wall, blocks - 1, sides))

    def link(src, dst, send, recv, k, device):
        return pltpu.make_async_remote_copy(
            src_ref=src, dst_ref=dst, send_sem=send.at[k], recv_sem=recv.at[k],
            device_id=device, device_id_type=MESH,
        )

    def wall_link(k):
        return link(wall_out.at[k], wall_in.at[k], wall_send, wall_recv, k, peer(k))

    def back_link(k):
        return link(back_out.at[k], back_in.at[k], back_send, back_recv, k, peer_back(k))

    @pl.when(on_wall)
    def _():
        mixed = out_low1[...]
        swapped = jnp.where(
            iota(mixed.shape, 0) % 2 == 0, pltpu.roll(mixed, ROWS - 1, 0), pltpu.roll(mixed, 1, 0)
        )
        temps = jnp.where(iota(mixed.shape, 1) % 2 == 0, swapped, mixed)
        owners = owner_v[...]
        targets = target_v[...].astype(F32)

        def masked(k, out):
            out[k, :ROWS] = temps
            out[k, ROWS:] = jnp.where(owners == lax.rem(gx + k, blocks), targets, -1.0)

        def step(k, carry):
            masked(k, wall_out)
            wall_link(k).start()
            return carry

        masked(0, wall_in)
        lax.fori_loop(1, blocks, step, 0)

    side_row = pl.multiple_of(jnp.where(core == 0, CY - 8, 0), 8)

    def faces(send, recv, side_from, out_up, in_up, out_down, in_down, side, out_low, in_low, out_high, in_high,
              fin_from, fin_to, fin_low, fin_high, fin_side, sent_fin_low, sent_fin_high, sent_fin_side):
        links = {
            FLUID_ABOVE: (link(out_high, in_low, send, recv, FLUID_ABOVE, above), has_above, has_below),
            FLUID_BELOW: (link(out_low, in_high, send, recv, FLUID_BELOW, below), has_below, has_above),
            FIN_UP: (link(sent_fin_high, fin_low, send, recv, FIN_UP, right), has_high, has_low),
            FIN_DOWN: (link(sent_fin_low, fin_high, send, recv, FIN_DOWN, left), has_low, has_high),
            FIN_SIDE: (link(sent_fin_side, fin_side, send, recv, FIN_SIDE, other), None, None),
            FIN_ABOVE: (link(fin_from.at[FD], fin_to.at[0], send, recv, FIN_ABOVE, above), has_above, has_below),
            FIN_BELOW: (link(fin_from.at[1], fin_to.at[FD + 1], send, recv, FIN_BELOW, below), has_below, has_above),
        }
        for half in range(2):
            up, down, across = FLUID_UP[half], FLUID_DOWN[half], FLUID_SIDE[half]
            lanes = pl.ds(half * 128, 128)
            rim = side_from.at[pl.ds(1, PAIRS), pl.ds(side_row, 8), lanes]
            links[up] = (link(out_up.at[half], in_up.at[half], send, recv, up, right), has_high, has_low)
            links[down] = (link(out_down.at[half], in_down.at[half], send, recv, down, left), has_low, has_high)
            links[across] = (link(rim, side.at[:, :, lanes], send, recv, across, other), None, None)
        return links

    def when(condition, action):
        if condition is None:
            action()
        else:
            pl.when(condition)(action)

    one = faces(send1, recv1, black, out_up1, in_up1, out_down1, in_down1, side1, out_low1, in_low1, out_high1, in_high1,
                fin_v, fin_v, fin_low1, fin_high1, fin_side1, out_fin_low1, out_fin_high1, out_fin_side1)
    two = faces(send2, recv2, red, out_up2, in_up2, out_down2, in_down2, side2, out_low2, in_low2, out_high2, in_high2,
                first, first, fin_low2, fin_high2, fin_side2, out_fin_low2, out_fin_high2, out_fin_side2)

    def start(links, *which):
        for k in which:
            when(links[k][1], links[k][0].start)

    def arrived(links, *which):
        for k in which:
            when(links[k][2], links[k][0].wait_recv)

    def sent(links):
        for k in range(FACES):
            when(links[k][1], links[k][0].wait_send)

    start(one, *FLUID_UP, *FLUID_DOWN, *FLUID_SIDE, FLUID_ABOVE, FLUID_BELOW)

    loads[3].wait()
    start(one, FIN_ABOVE, FIN_BELOW)

    def pack_fin(group, carry):
        low = high = jnp.zeros((8, FH), F32)
        for k in range(8):
            plane = fin_v[group * 8 + k + 1]
            low, high = pick_rows(k, plane, low, high)
            pick_side(group * 8 + k, plane, out_fin_side1, core)
        out_fin_low1[group] = low
        out_fin_high1[group] = high
        return carry

    lax.fori_loop(0, FD // 8, pack_fin, 0)
    start(one, FIN_SIDE, FIN_UP, FIN_DOWN)

    loads[4].wait()
    loads[5].wait()
    arrived(one, *FLUID_SIDE, FLUID_ABOVE, FLUID_BELOW)
    low1[...] = as_columns(in_low1[...])
    high1[...] = as_columns(in_high1[...])

    def red_step(pair, carry):
        def put(rows, sources, new):
            red[pair + 1, rows] = new
            pick_low(2 * pair, new, low_column, rows)
            pick_high(2 * pair, new, high_column, rows)

        half_sweep(pair, black, red, active_v, side1, low1, high1, True, core, put)
        return carry

    lax.fori_loop(1, PAIRS - 1, red_step, 0)

    @pl.when(on_wall)
    def _():
        cells = (ROWS, CY)
        least = (2 * FH * iota(cells, 0) + 2 * iota(cells, 1)).astype(F32)
        roots = fin_v[1]
        surface = []
        for di in range(2):
            for dj in range(2):
                columns = dot(roots, spread(FH, CY, dj, 0))
                surface.append(dot(spread(ROWS, FW, di, 1), columns))
        shifts = (0.0, 1.0, float(FH), float(FH + 1))

        def owned(k, sums):
            offset = wall_in[k, ROWS:] - least
            temps = wall_in[k, :ROWS]
            value = jnp.zeros(cells, F32)
            new = []
            for part, shift, total in zip(surface, shifts, sums):
                hit = offset == shift
                value = jnp.where(hit, part, value)
                new.append(total + jnp.where(hit, temps - part, 0.0))
            back_out[k] = value
            return tuple(new)

        def step(k, sums):
            wall_link(k).wait_recv()
            sums = owned(k, sums)
            back_link(k).start()
            return sums

        sums = owned(0, (jnp.zeros(cells, F32),) * 4)
        sums = lax.fori_loop(1, blocks, step, sums)
        deposit = jnp.zeros((FW, FH), F32)
        for di in range(2):
            rows = spread(FW, ROWS, di, 0)
            for dj in range(2):
                deposit = deposit + dot(
                    dot(rows, sums[2 * di + dj]), spread(CY, FH, dj, 1)
                )
        fin_v[0] = deposit
        first[0] = deposit

    def unfold(arrived_up, arrived_down, field):
        def low_plane():
            for half in range(2):
                field[0, :, half * 128 : half * 128 + 128] = both_halves(arrived_up[half])

        def high_plane():
            for half in range(2):
                field[PAIRS + 1, :, half * 128 : half * 128 + 128] = both_halves(arrived_down[half])

        when(has_low, low_plane)
        when(has_high, high_plane)

    arrived(one, *FLUID_UP, *FLUID_DOWN)
    unfold(in_up1, in_down1, black)
    red_step(0, 0)
    red_step(PAIRS - 1, 0)
    out_low2[...] = as_rows(low_column[...])
    out_high2[...] = as_rows(high_column[...])
    fold(red, PAIRS - 1, 1, out_up2, 1)
    fold(red, 0, 0, out_down2, 1)
    start(two, FLUID_UP[1], FLUID_DOWN[1], FLUID_SIDE[1], FLUID_ABOVE, FLUID_BELOW)

    arrived(one, FIN_SIDE, FIN_UP, FIN_DOWN, FIN_BELOW, FIN_ABOVE)

    def fin_step(group, carry):
        low = high = jnp.zeros((8, FH), F32)
        for k in range(8):
            d = group * 8 + k
            here, total = fin_sum(group, k, fin_v, fin_low1, fin_high1, fin_side1, core)
            rhs = here + source_v[d]
            new = (rhs + total) * SEVENTH
            first[d + 1] = new
            base[d] = (OMEGA * SEVENTH) * rhs + (1.0 - OMEGA) * here
            low, high = pick_rows(k, new, low, high)
            pick_side(d, new, out_fin_side2, core)
        out_fin_low2[group] = low
        out_fin_high2[group] = high
        return carry

    lax.fori_loop(0, FD // 8, fin_step, 0)
    start(two, FIN_UP, FIN_DOWN, FIN_SIDE, FIN_ABOVE, FIN_BELOW)

    @pl.when(on_wall)
    def _():
        def step(k, total):
            back_link(k).wait_recv()
            return total + back_in[k]

        ghost = lax.fori_loop(1, blocks, step, back_out[0])
        later = pltpu.roll(ghost, ROWS - 1, 0)
        even_cell = iota(ghost.shape, 1) % 2 == 0
        in_low2[...] = jnp.where(even_cell, later, ghost)
        low2[...] = as_columns(jnp.where(even_cell, ghost, later))

        def fix(pair, carry):
            x = 2 * pair
            lane = iota((CY, 128), 1)
            even = parity_rows((CY, 128)) == 0
            on = jnp.where(even, active_v[x, :, :128], active_v[x + 1, :, :128]) == 1
            share = pltpu.roll(low2[...], (128 - x) % 128, 1) * SEVENTH
            half = red[pair + 1, :, :128]
            red[pair + 1, :, :128] = half + jnp.where(on & (lane == 0), share, 0.0)
            return carry

        lax.fori_loop(0, PAIRS, fix, 0)

    fold(red, PAIRS - 1, 1, out_up2, 0)
    fold(red, 0, 0, out_down2, 0)
    start(two, FLUID_UP[0], FLUID_DOWN[0], FLUID_SIDE[0])

    sent(one)

    @pl.when(on_wall)
    def _():
        def step(k, carry):
            wall_link(k).wait_send()
            back_link(k).wait_send()
            return carry

        lax.fori_loop(1, blocks, step, 0)

    arrived(two, FIN_UP, FIN_DOWN, FIN_SIDE, FIN_ABOVE, FIN_BELOW)

    def fin_again(group, carry):
        for k in range(8):
            d = group * 8 + k
            _, total = fin_sum(group, k, first, fin_low2, fin_high2, fin_side2, core)
            base[d] = base[d] + (OMEGA * SEVENTH) * total
        return carry

    lax.fori_loop(0, FD // 8, fin_again, 0)

    arrived(two, *FLUID_UP, *FLUID_DOWN, *FLUID_SIDE, FLUID_ABOVE, FLUID_BELOW)
    low2[...] = as_columns(in_low2[...])
    high2[...] = as_columns(in_high2[...])
    unfold(in_up2, in_down2, red)
    sent(two)


def second_kernel(red, black, active, fin_new, side, low, high, fluid_out, fin_out, fluid_v, fluid_sem, fin_sem):
    core = lax.axis_index("gy")
    fin_copy = pltpu.make_async_copy(fin_new, fin_out, fin_sem)
    fin_copy.start()

    def fluid_copy(pair):
        planes = pl.ds(2 * pair, 2)
        return pltpu.make_async_copy(fluid_v.at[planes], fluid_out.at[planes], fluid_sem.at[pair])

    def black_step(pair, carry):
        def put(rows, reds, new):
            even = parity_rows(new.shape) == 0
            fluid_v[2 * pair, rows] = jnp.where(even, reds, new)
            fluid_v[2 * pair + 1, rows] = jnp.where(even, new, reds)

        half_sweep(pair, red, black, active, side, low, high, False, core, put)
        fluid_copy(pair).start()
        return carry

    lax.fori_loop(0, PAIRS, black_step, 0)

    def done(pair, carry):
        fluid_copy(pair).wait()
        return carry

    lax.fori_loop(0, PAIRS, done, 0)
    fin_copy.wait()


def local(sizes, fluid_temp, active, fin_temp, fin_source, wall_owner, wall_target):
    blocks = sizes[1]
    owner = wall_owner.reshape(CX, CY)
    target = wall_target.reshape(CX, CY)
    anywhere = pl.BlockSpec(memory_space=pl.ANY)
    vmem = pl.BlockSpec(memory_space=pltpu.VMEM)
    column, rows, strip = (CY, 128), (FD // 8, 8, FH), (FW, 128)
    packed, rim = (PAIRS + 2, CY, CZ), (PAIRS, 8, CZ)
    held = [
        pltpu.VMEM(packed, F32),
        pltpu.VMEM(packed, F32),
        pltpu.VMEM((CX, CY, CZ), jnp.int32),
        *[pltpu.VMEM(s, F32) for s in ((FD, FW, FH), rim, column, column)],
    ]
    dma = pltpu.SemaphoreType.DMA
    in_hbm = [
        pltpu.with_memory_space_constraint(x, pltpu.HBM)
        for x in (fluid_temp, active, fin_temp, fin_source, owner, target)
    ]
    middle = pl.pallas_call(
        functools.partial(exchange_kernel, sizes),
        name="exchange_and_first_sweeps",
        out_shape=held,
        in_specs=[anywhere] * 6,
        out_specs=[vmem] * 7,
        scratch_shapes=[
            pltpu.VMEM((CX, CY, CZ), F32),
            pltpu.VMEM((FD + 2, FW, FH), F32),
            pltpu.VMEM((FD + 2, FW, FH), F32),
            pltpu.VMEM((FD, FW, FH), F32),
            pltpu.VMEM((CX, CY), jnp.int32),
            pltpu.VMEM((CX, CY), jnp.int32),
            *[pltpu.VMEM(s, F32) for s in (rim, column, column, rows, rows, strip)],
            *[pltpu.VMEM(s, F32) for s in (rows, rows, strip)],
            *[pltpu.VMEM(s, F32) for s in (rows, rows, strip)],
            *[pltpu.VMEM(s, F32) for s in (rows, rows, strip)],
            *[pltpu.VMEM(column, F32) for _ in range(2)],
            *[pltpu.VMEM((ROWS, CY), F32) for _ in range(8)],
            *[pltpu.VMEM((2, HALF, 128), F32) for _ in range(8)],
            pltpu.VMEM((blocks, 2 * ROWS, CY), F32),
            pltpu.VMEM((blocks, 2 * ROWS, CY), F32),
            pltpu.VMEM((blocks, ROWS, CY), F32),
            pltpu.VMEM((blocks, ROWS, CY), F32),
            dma((6,)),
            *[dma((FACES,)) for _ in range(4)],
            *[dma((blocks,)) for _ in range(4)],
        ],
        compiler_params=pltpu.CompilerParams(
            collective_id=0, has_side_effects=True, vmem_limit_bytes=40 * 2**20
        ),
    )(*in_hbm)
    return pl.pallas_call(
        second_kernel,
        name="second_sweeps",
        out_shape=[
            jax.ShapeDtypeStruct((CX, CY, CZ), F32),
            jax.ShapeDtypeStruct((FD, FW, FH), F32),
        ],
        in_specs=[vmem] * 7,
        out_specs=[anywhere] * 2,
        scratch_shapes=[
            pltpu.VMEM((CX, CY, CZ), F32),
            dma((PAIRS,)),
            dma,
        ],
        compiler_params=pltpu.CompilerParams(vmem_limit_bytes=40 * 2**20),
    )(*middle)


def solution(mesh):
    in_specs = (
        P("gx", "gy", "grp"),
        P("gx", "gy", "grp"),
        P("grp", "gx", "gy"),
        P("grp", "gx", "gy"),
        P("gx", "gy", None, None),
        P("gx", "gy", None),
    )
    out_specs = (P("gx", "gy", "grp"), P("grp", "gx", "gy"))
    sizes = (mesh.shape["grp"], mesh.shape["gx"])
    body = functools.partial(local, sizes)
    return jax.shard_map(body, mesh=mesh, in_specs=in_specs, out_specs=out_specs, check_vma=False)
```

```python
import functools

import jax
import jax.numpy as jnp
from jax import lax
from jax.experimental import pallas as pl
from jax.experimental.pallas import tpu as pltpu
from jax.sharding import PartitionSpec as P

F32 = jnp.float32
MESH = pl.DeviceIdType.MESH
DIAG = 7.0
SPECTRAL = 6.0 / DIAG
OMEGA = 1.0 / (1.0 - SPECTRAL * SPECTRAL / 2.0)
SEVENTH = 1.0 / 7.0

CX, CY, CZ = 16, 128, 256
FD, FW, FH = 64, 32, 256
ROWS = CX

HALF = CY // 2
PAIRS = CX // 2
CHUNK = 32

FLUID_UP, FLUID_DOWN, FLUID_SIDE = (0, 1), (2, 3), (4, 5)
FLUID_ABOVE, FLUID_BELOW = 6, 7
FIN_UP, FIN_DOWN, FIN_SIDE, FIN_ABOVE, FIN_BELOW = 8, 9, 10, 11, 12
FACES = 13


def iota(shape, axis):
    return lax.broadcasted_iota(jnp.int32, shape, axis)


def parity_rows(shape):
    rows, lanes = shape
    tile = (iota((8, lanes), 0) + iota((8, lanes), 1)) % 2
    return jnp.concatenate([tile] * (rows // 8), axis=0)


def shifted_rows(plane, low_tile, high_tile):
    rows, lanes = plane.shape
    sub = iota((8, lanes), 0)
    up = pltpu.roll(plane, 1, 0)
    down = pltpu.roll(plane, rows - 1, 0)
    up = jnp.concatenate([jnp.where(sub == 0, low_tile, up[:8]), up[8:]], axis=0)
    down = jnp.concatenate([down[:-8], jnp.where(sub == 7, high_tile, down[-8:])], axis=0)
    return up + down


def shifted_lanes(plane, low_tile, high_tile):
    rows, lanes = plane.shape
    lane = iota((rows, 128), 1)
    left = pltpu.roll(plane, 1, 1)
    right = pltpu.roll(plane, lanes - 1, 1)
    first = jnp.where(lane == 0, low_tile, left[:, :128]) + right[:, :128]
    last = left[:, 128:] + jnp.where(lane == 127, high_tile, right[:, 128:])
    return jnp.concatenate([first, last], axis=1)


def half_sweep(pair, source, target, active, side, low, high, red, core, put):
    x = 2 * pair
    for start in range(0, CY, CHUNK):
        rows = slice(start, start + CHUNK)
        even = parity_rows((CHUNK, CZ)) == 0
        here = source[pair + 1, rows]
        before, after = source[pair, rows], source[pair + 2, rows]
        near, far = active[x, rows], active[x + 1, rows]
        if red:
            total = here + jnp.where(even, before, after)
            on = jnp.where(even, near, far) == 1
        else:
            total = here + jnp.where(even, after, before)
            on = jnp.where(even, far, near) == 1
        if start == 0:
            low_tile = jnp.where(core == 1, pltpu.roll(side[pair], 1, 0), 0.0)
        else:
            low_tile = pltpu.roll(source[pair + 1, start - 8 : start], 1, 0)
        stop = start + CHUNK
        if stop == CY:
            high_tile = jnp.where(core == 0, pltpu.roll(side[pair], 7, 0), 0.0)
        else:
            high_tile = pltpu.roll(source[pair + 1, stop : stop + 8], 7, 0)
        total = total + shifted_rows(here, low_tile, high_tile)
        low_lane = pltpu.roll(low[rows], (128 - x) % 128, 1)
        high_lane = pltpu.roll(high[rows], 127 - x, 1)
        total = total + shifted_lanes(here, low_lane, high_lane)
        old = target[pair + 1, rows]
        put(rows, here, jnp.where(on, (old + total) * SEVENTH, old))


def fin_sum(group, k, field, low, high, side, core):
    d = group * 8 + k
    here = field[d + 1]
    total = field[d] + field[d + 2]
    low_tile = pltpu.roll(low[group], (8 - k) % 8, 0)
    high_tile = pltpu.roll(high[group], 7 - k, 0)
    total = total + shifted_rows(here, low_tile, high_tile)
    column = pltpu.roll(side[...], jnp.where(core == 1, (128 - d) % 128, 127 - d), 1)
    total = total + shifted_lanes(
        here, jnp.where(core == 1, column, 0.0), jnp.where(core == 0, column, 0.0)
    )
    return here, total


def pick_low(x, plane, low, rows=slice(None)):
    lane = iota((plane.shape[0], 128), 1)
    low[rows] = jnp.where(lane == x, pltpu.roll(plane[:, :128], x, 1), low[rows])


def pick_high(x, plane, high, rows=slice(None)):
    lane = iota((plane.shape[0], 128), 1)
    high[rows] = jnp.where(lane == x, pltpu.roll(plane[:, 128:], (x + 1) % 128, 1), high[rows])


def one_colour(plane, colour):
    folded = pltpu.roll(plane[HALF:], HALF - 1, 0)
    return jnp.where(parity_rows(folded.shape) == colour, plane[:HALF], folded)


def both_halves(folded):
    return jnp.concatenate([folded, pltpu.roll(folded, 1, 0)], axis=0)


def as_rows(columns):
    return jnp.transpose(columns)[:ROWS]


def as_columns(rows):
    square = jnp.concatenate([rows, jnp.zeros((CY - ROWS, CY), F32)], axis=0)
    return jnp.transpose(square)


def pick_rows(k, plane, low, high):
    sub = iota((8, plane.shape[1]), 0)
    low = jnp.where(sub == k, pltpu.roll(plane[:8], k, 0), low)
    high = jnp.where(sub == k, pltpu.roll(plane[-8:], (k + 1) % 8, 0), high)
    return low, high


def pick_side(d, plane, out, core):
    lane = iota((plane.shape[0], 128), 1)
    half = jnp.where(core == 0, plane[:, 128:], plane[:, :128])
    turned = pltpu.roll(half, jnp.where(core == 0, (d + 1) % 128, d), 1)
    out[...] = jnp.where(lane == d, turned, out[...])


def spread(rows, columns, offset, axis):
    a, b = iota((rows, columns), axis), iota((rows, columns), 1 - axis)
    return jnp.where(a == 2 * b + offset, 1.0, 0.0).astype(F32)


def dot(a, b):
    return jnp.dot(a, b, precision=lax.Precision.HIGHEST, preferred_element_type=F32)


def exchange_kernel(
    sizes,
    fluid, active, fin, source, owner, target,
    red, black, active_v, base, side2, low2, high2,
    fluid_v, fin_v, first, source_v, owner_v, target_v,
    side1, low1, high1, fin_low1, fin_high1, fin_side1, fin_low2, fin_high2, fin_side2,
    out_fin_low1, out_fin_high1, out_fin_side1, out_fin_low2, out_fin_high2, out_fin_side2,
    low_column, high_column,
    out_low1, out_high1, in_low1, in_high1, out_low2, out_high2, in_low2, in_high2,
    out_up1, out_down1, in_up1, in_down1, out_up2, out_down2, in_up2, in_down2,
    wall_out, wall_in, temps_out, temps_in, back_out, back_in, surface,
    load_sem, send1, recv1, send2, recv2, wall_send, wall_recv, temps_send, temps_recv, back_send, back_recv,
):
    groups, blocks = sizes
    grp, gx, core = lax.axis_index("grp"), lax.axis_index("gx"), lax.axis_index("gy")
    has_low, has_high = gx > 0, gx < blocks - 1
    has_below, has_above = grp > 0, grp < groups - 1
    on_wall = grp == 0
    left, right = (grp, gx - 1, core), (grp, gx + 1, core)
    below, above = (grp - 1, gx, core), (grp + 1, gx, core)
    other = (grp, gx, 1 - core)

    def wrapped(index):
        return jnp.where(index >= blocks, index - blocks, index)

    def peer(k):
        return (grp, wrapped(gx + k), core)

    def peer_back(k):
        return (grp, wrapped(gx - k + blocks), core)

    load_owner = pltpu.make_async_copy(owner, owner_v, load_sem.at[0])
    load_target = pltpu.make_async_copy(target, target_v, load_sem.at[1])
    load_fin = pltpu.make_async_copy(fin, fin_v.at[pl.ds(1, FD)], load_sem.at[2])
    load_fluid = pltpu.make_async_copy(fluid, fluid_v, load_sem.at[3])
    load_source = pltpu.make_async_copy(source, source_v, load_sem.at[4])
    load_active = pltpu.make_async_copy(active, active_v, load_sem.at[5])
    loads = (load_owner, load_target, load_fin, load_fluid, load_source, load_active)
    for load in loads:
        load.start()

    barrier = pltpu.get_barrier_semaphore()

    def greet(device):
        pl.semaphore_signal(barrier, inc=1, device_id=device, device_id_type=MESH)

    greet(other)

    @pl.when(has_above)
    def _():
        greet(above)

    @pl.when(has_below)
    def _():
        greet(below)

    @pl.when(on_wall)
    def _():
        def step(k, carry):
            greet(peer(k))
            return carry

        lax.fori_loop(1, blocks, step, 0)

    @pl.when(jnp.logical_not(on_wall) & has_low)
    def _():
        greet(left)

    @pl.when(jnp.logical_not(on_wall) & has_high)
    def _():
        greet(right)

    @pl.when(jnp.logical_not(has_low))
    def _():
        black[0] = jnp.zeros((CY, CZ), F32)
        red[0] = jnp.zeros((CY, CZ), F32)
        fin_low1[...] = jnp.zeros(fin_low1.shape, F32)
        fin_low2[...] = jnp.zeros(fin_low2.shape, F32)

    @pl.when(jnp.logical_not(has_high))
    def _():
        black[PAIRS + 1] = jnp.zeros((CY, CZ), F32)
        red[PAIRS + 1] = jnp.zeros((CY, CZ), F32)
        fin_high1[...] = jnp.zeros(fin_high1.shape, F32)
        fin_high2[...] = jnp.zeros(fin_high2.shape, F32)

    @pl.when(jnp.logical_not(has_below))
    def _():
        in_low1[...] = jnp.zeros(in_low1.shape, F32)

    @pl.when(jnp.logical_not(has_above))
    def _():
        in_high1[...] = jnp.zeros(in_high1.shape, F32)
        in_high2[...] = jnp.zeros(in_high2.shape, F32)
        fin_v[FD + 1] = jnp.zeros((FW, FH), F32)
        first[FD + 1] = jnp.zeros((FW, FH), F32)

    for ref in (low_column, high_column, out_fin_side1, out_fin_side2):
        ref[...] = jnp.zeros(ref.shape, F32)

    load_fin.wait()

    def pack_fin(group, carry):
        low = high = jnp.zeros((8, FH), F32)
        for k in range(8):
            plane = fin_v[group * 8 + k + 1]
            low, high = pick_rows(k, plane, low, high)
            pick_side(group * 8 + k, plane, out_fin_side1, core)
        out_fin_low1[group] = low
        out_fin_high1[group] = high
        return carry

    lax.fori_loop(0, FD // 8, pack_fin, 0)
    load_owner.wait()
    load_target.wait()

    expected = 1 + has_above.astype(jnp.int32) + has_below.astype(jnp.int32)
    sides = has_low.astype(jnp.int32) + has_high.astype(jnp.int32)
    pl.semaphore_wait(barrier, expected + jnp.where(on_wall, blocks - 1, sides))

    def link(src, dst, send, recv, k, device):
        return pltpu.make_async_remote_copy(
            src_ref=src, dst_ref=dst, send_sem=send.at[k], recv_sem=recv.at[k],
            device_id=device, device_id_type=MESH,
        )

    def wall_link(k):
        return link(wall_out.at[k], wall_in.at[k], wall_send, wall_recv, k, peer(k))

    def back_link(k):
        return link(back_out.at[k], back_in.at[k], back_send, back_recv, k, peer_back(k))

    def temps_link(k):
        return link(temps_out, temps_in.at[k], temps_send, temps_recv, k, peer(k))

    @pl.when(on_wall)
    def _():
        owners = owner_v[...]
        targets = target_v[...].astype(F32)

        def owned_by(k):
            return jnp.where(owners == wrapped(gx + k), targets, -1.0)

        def step(k, carry):
            wall_out[k] = owned_by(k)
            wall_link(k).start()
            return carry

        wall_in[0] = owned_by(0)
        lax.fori_loop(1, blocks, step, 0)

    side_row = pl.multiple_of(jnp.where(core == 0, CY - 8, 0), 8)

    def faces(send, recv, side_from, out_up, in_up, out_down, in_down, side, out_low, in_low, out_high, in_high,
              fin_from, fin_to, fin_low, fin_high, fin_side, sent_fin_low, sent_fin_high, sent_fin_side):
        links = {
            FLUID_ABOVE: (link(out_high, in_low, send, recv, FLUID_ABOVE, above), has_above, has_below),
            FLUID_BELOW: (link(out_low, in_high, send, recv, FLUID_BELOW, below), has_below, has_above),
            FIN_UP: (link(sent_fin_high, fin_low, send, recv, FIN_UP, right), has_high, has_low),
            FIN_DOWN: (link(sent_fin_low, fin_high, send, recv, FIN_DOWN, left), has_low, has_high),
            FIN_SIDE: (link(sent_fin_side, fin_side, send, recv, FIN_SIDE, other), None, None),
            FIN_ABOVE: (link(fin_from.at[FD], fin_to.at[0], send, recv, FIN_ABOVE, above), has_above, has_below),
            FIN_BELOW: (link(fin_from.at[1], fin_to.at[FD + 1], send, recv, FIN_BELOW, below), has_below, has_above),
        }
        for half in range(2):
            up, down, across = FLUID_UP[half], FLUID_DOWN[half], FLUID_SIDE[half]
            lanes = pl.ds(half * 128, 128)
            rim = side_from.at[pl.ds(1, PAIRS), pl.ds(side_row, 8), lanes]
            links[up] = (link(out_up.at[half], in_up.at[half], send, recv, up, right), has_high, has_low)
            links[down] = (link(out_down.at[half], in_down.at[half], send, recv, down, left), has_low, has_high)
            links[across] = (link(rim, side.at[:, :, lanes], send, recv, across, other), None, None)
        return links

    def when(condition, action):
        if condition is None:
            action()
        else:
            pl.when(condition)(action)

    one = faces(send1, recv1, black, out_up1, in_up1, out_down1, in_down1, side1, out_low1, in_low1, out_high1, in_high1,
                fin_v, fin_v, fin_low1, fin_high1, fin_side1, out_fin_low1, out_fin_high1, out_fin_side1)
    two = faces(send2, recv2, red, out_up2, in_up2, out_down2, in_down2, side2, out_low2, in_low2, out_high2, in_high2,
                first, first, fin_low2, fin_high2, fin_side2, out_fin_low2, out_fin_high2, out_fin_side2)

    def start(links, *which):
        for k in which:
            when(links[k][1], links[k][0].start)

    def arrived(links, *which):
        for k in which:
            when(links[k][2], links[k][0].wait_recv)

    def sent(links):
        for k in range(FACES):
            when(links[k][1], links[k][0].wait_send)

    start(one, FIN_SIDE, FIN_UP, FIN_DOWN, FIN_ABOVE, FIN_BELOW)

    load_fluid.wait()

    def pack_fluid(pair, carry):
        x = 2 * pair
        for start in range(0, CY, CHUNK):
            rows = slice(start, start + CHUNK)
            even = parity_rows((CHUNK, CZ)) == 0
            near, far = fluid_v[x, rows], fluid_v[x + 1, rows]
            reds, blacks = jnp.where(even, near, far), jnp.where(even, far, near)
            red[pair + 1, rows] = reds
            black[pair + 1, rows] = blacks
            pick_low(x, blacks, low_column, rows)
            pick_low(x + 1, reds, low_column, rows)
            pick_high(x, blacks, high_column, rows)
        return carry

    lax.fori_loop(0, PAIRS, pack_fluid, 0)
    out_low1[...] = as_rows(low_column[...])
    out_high1[...] = as_rows(high_column[...])

    def fold(field, pair, colour, out, half):
        out[half] = one_colour(field[pair + 1, :, half * 128 : half * 128 + 128], colour)

    for half in range(2):
        fold(black, PAIRS - 1, 0, out_up1, half)
        fold(black, 0, 1, out_down1, half)

    start(one, *FLUID_UP, *FLUID_DOWN, *FLUID_SIDE, FLUID_ABOVE, FLUID_BELOW)

    @pl.when(on_wall)
    def _():
        mixed = out_low1[...]
        swapped = jnp.where(
            iota(mixed.shape, 0) % 2 == 0, pltpu.roll(mixed, ROWS - 1, 0), pltpu.roll(mixed, 1, 0)
        )
        temps = jnp.where(iota(mixed.shape, 1) % 2 == 0, swapped, mixed)
        temps_out[...] = temps
        temps_in[0] = temps

        def step(k, carry):
            temps_link(k).start()
            return carry

        lax.fori_loop(1, blocks, step, 0)

    cells = (ROWS, CY)
    shifts = (0.0, 1.0, float(FH), float(FH + 1))

    def offsets(k):
        return wall_in[k] - (2 * FH * iota(cells, 0) + 2 * iota(cells, 1)).astype(F32)

    @pl.when(on_wall)
    def _():
        roots = fin_v[1]
        columns = [dot(roots, spread(FH, CY, dj, 0)) for dj in range(2)]
        for di in range(2):
            for dj in range(2):
                surface[2 * di + dj] = dot(spread(ROWS, FW, di, 1), columns[dj])

        def answer(k):
            offset = offsets(k)
            value = jnp.zeros(cells, F32)
            for n, shift in enumerate(shifts):
                value = jnp.where(offset == shift, surface[n], value)
            back_out[k] = value

        def step(k, carry):
            wall_link(k).wait_recv()
            answer(k)
            back_link(k).start()
            return carry

        answer(0)
        lax.fori_loop(1, blocks, step, 0)

    load_source.wait()
    arrived(one, FIN_SIDE, FIN_UP, FIN_DOWN, FIN_BELOW, FIN_ABOVE)

    def fin_step(group, carry):
        low = high = jnp.zeros((8, FH), F32)
        for k in range(8):
            d = group * 8 + k
            here, total = fin_sum(group, k, fin_v, fin_low1, fin_high1, fin_side1, core)
            rhs = here + source_v[d]
            new = (rhs + total) * SEVENTH
            first[d + 1] = new
            base[d] = (OMEGA * SEVENTH) * rhs + (1.0 - OMEGA) * here
            low, high = pick_rows(k, new, low, high)
            pick_side(d, new, out_fin_side2, core)
        out_fin_low2[group] = low
        out_fin_high2[group] = high
        return carry

    lax.fori_loop(1, FD // 8, fin_step, 0)

    @pl.when(on_wall)
    def _():
        def owned(k, sums):
            offset = offsets(k)
            flux = temps_in[k] - back_out[k]
            return tuple(
                total + jnp.where(offset == shift, flux, 0.0) for shift, total in zip(shifts, sums)
            )

        def step(k, sums):
            temps_link(k).wait_recv()
            return owned(k, sums)

        sums = owned(0, (jnp.zeros(cells, F32),) * 4)
        sums = lax.fori_loop(1, blocks, step, sums)
        deposit = jnp.zeros((FW, FH), F32)
        for dj in range(2):
            rows = dot(spread(FW, ROWS, 0, 0), sums[dj]) + dot(spread(FW, ROWS, 1, 0), sums[2 + dj])
            deposit = deposit + dot(rows, spread(CY, FH, dj, 1))
        fin_v[0] = deposit
        first[0] = deposit

    fin_step(0, 0)
    start(two, FIN_UP, FIN_DOWN, FIN_SIDE, FIN_ABOVE, FIN_BELOW)

    load_active.wait()
    arrived(one, *FLUID_UP, *FLUID_DOWN, *FLUID_SIDE, FLUID_ABOVE, FLUID_BELOW)
    low1[...] = as_columns(in_low1[...])
    high1[...] = as_columns(in_high1[...])

    def red_step(pair, carry):
        def put(rows, sources, new):
            red[pair + 1, rows] = new
            pick_low(2 * pair, new, low_column, rows)
            pick_high(2 * pair, new, high_column, rows)

        half_sweep(pair, black, red, active_v, side1, low1, high1, True, core, put)
        return carry

    def unfold(arrived_up, arrived_down, field):
        def low_plane():
            for half in range(2):
                field[0, :, half * 128 : half * 128 + 128] = both_halves(arrived_up[half])

        def high_plane():
            for half in range(2):
                field[PAIRS + 1, :, half * 128 : half * 128 + 128] = both_halves(arrived_down[half])

        when(has_low, low_plane)
        when(has_high, high_plane)

    unfold(in_up1, in_down1, black)
    lax.fori_loop(0, PAIRS, red_step, 0)
    out_low2[...] = as_rows(low_column[...])
    out_high2[...] = as_rows(high_column[...])
    fold(red, PAIRS - 1, 1, out_up2, 1)
    fold(red, 0, 0, out_down2, 1)
    start(two, FLUID_UP[1], FLUID_DOWN[1], FLUID_SIDE[1], FLUID_ABOVE, FLUID_BELOW)

    @pl.when(on_wall)
    def _():
        def step(k, total):
            back_link(k).wait_recv()
            return total + back_in[k]

        ghost = lax.fori_loop(1, blocks, step, back_out[0])
        later = pltpu.roll(ghost, ROWS - 1, 0)
        even_cell = iota(ghost.shape, 1) % 2 == 0
        in_low2[...] = jnp.where(even_cell, later, ghost)
        low2[...] = as_columns(jnp.where(even_cell, ghost, later))

        def fix(pair, carry):
            x = 2 * pair
            lane = iota((CY, 128), 1)
            even = parity_rows((CY, 128)) == 0
            on = jnp.where(even, active_v[x, :, :128], active_v[x + 1, :, :128]) == 1
            share = pltpu.roll(low2[...], (128 - x) % 128, 1) * SEVENTH
            half = red[pair + 1, :, :128]
            red[pair + 1, :, :128] = half + jnp.where(on & (lane == 0), share, 0.0)
            return carry

        lax.fori_loop(0, PAIRS, fix, 0)

    fold(red, PAIRS - 1, 1, out_up2, 0)
    fold(red, 0, 0, out_down2, 0)
    start(two, FLUID_UP[0], FLUID_DOWN[0], FLUID_SIDE[0])

    sent(one)

    @pl.when(on_wall)
    def _():
        def step(k, carry):
            wall_link(k).wait_send()
            temps_link(k).wait_send()
            back_link(k).wait_send()
            return carry

        lax.fori_loop(1, blocks, step, 0)

    arrived(two, FIN_UP, FIN_DOWN, FIN_SIDE, FIN_ABOVE, FIN_BELOW)

    def fin_again(group, carry):
        for k in range(8):
            d = group * 8 + k
            _, total = fin_sum(group, k, first, fin_low2, fin_high2, fin_side2, core)
            base[d] = base[d] + (OMEGA * SEVENTH) * total
        return carry

    lax.fori_loop(0, FD // 8, fin_again, 0)

    arrived(two, *FLUID_UP, *FLUID_DOWN, *FLUID_SIDE, FLUID_ABOVE, FLUID_BELOW)
    low2[...] = as_columns(in_low2[...])
    high2[...] = as_columns(in_high2[...])
    unfold(in_up2, in_down2, red)
    sent(two)


def second_kernel(red, black, active, fin_new, side, low, high, fluid_out, fin_out, fluid_v, fluid_sem, fin_sem):
    core = lax.axis_index("gy")
    fin_copy = pltpu.make_async_copy(fin_new, fin_out, fin_sem)
    fin_copy.start()

    def fluid_copy(pair):
        planes = pl.ds(2 * pair, 2)
        return pltpu.make_async_copy(fluid_v.at[planes], fluid_out.at[planes], fluid_sem.at[pair])

    def black_step(pair, carry):
        def put(rows, reds, new):
            even = parity_rows(new.shape) == 0
            fluid_v[2 * pair, rows] = jnp.where(even, reds, new)
            fluid_v[2 * pair + 1, rows] = jnp.where(even, new, reds)

        half_sweep(pair, red, black, active, side, low, high, False, core, put)
        fluid_copy(pair).start()
        return carry

    lax.fori_loop(0, PAIRS, black_step, 0)

    def done(pair, carry):
        fluid_copy(pair).wait()
        return carry

    lax.fori_loop(0, PAIRS, done, 0)
    fin_copy.wait()


def local(sizes, fluid_temp, active, fin_temp, fin_source, wall_owner, wall_target):
    blocks = sizes[1]
    owner = wall_owner.reshape(CX, CY)
    target = wall_target.reshape(CX, CY)
    anywhere = pl.BlockSpec(memory_space=pl.ANY)
    vmem = pl.BlockSpec(memory_space=pltpu.VMEM)
    column, rows, strip = (CY, 128), (FD // 8, 8, FH), (FW, 128)
    packed, rim = (PAIRS + 2, CY, CZ), (PAIRS, 8, CZ)
    held = [
        pltpu.VMEM(packed, F32),
        pltpu.VMEM(packed, F32),
        pltpu.VMEM((CX, CY, CZ), jnp.int32),
        *[pltpu.VMEM(s, F32) for s in ((FD, FW, FH), rim, column, column)],
    ]
    dma = pltpu.SemaphoreType.DMA
    in_hbm = [
        pltpu.with_memory_space_constraint(x, pltpu.HBM)
        for x in (fluid_temp, active, fin_temp, fin_source, owner, target)
    ]
    middle = pl.pallas_call(
        functools.partial(exchange_kernel, sizes),
        name="exchange_and_first_sweeps",
        out_shape=held,
        in_specs=[anywhere] * 6,
        out_specs=[vmem] * 7,
        scratch_shapes=[
            pltpu.VMEM((CX, CY, CZ), F32),
            pltpu.VMEM((FD + 2, FW, FH), F32),
            pltpu.VMEM((FD + 2, FW, FH), F32),
            pltpu.VMEM((FD, FW, FH), F32),
            pltpu.VMEM((CX, CY), jnp.int32),
            pltpu.VMEM((CX, CY), jnp.int32),
            *[pltpu.VMEM(s, F32) for s in (rim, column, column, rows, rows, strip)],
            *[pltpu.VMEM(s, F32) for s in (rows, rows, strip)],
            *[pltpu.VMEM(s, F32) for s in (rows, rows, strip)],
            *[pltpu.VMEM(s, F32) for s in (rows, rows, strip)],
            *[pltpu.VMEM(column, F32) for _ in range(2)],
            *[pltpu.VMEM((ROWS, CY), F32) for _ in range(8)],
            *[pltpu.VMEM((2, HALF, 128), F32) for _ in range(8)],
            pltpu.VMEM((blocks, ROWS, CY), F32),
            pltpu.VMEM((blocks, ROWS, CY), F32),
            pltpu.VMEM((ROWS, CY), F32),
            *[pltpu.VMEM((blocks, ROWS, CY), F32) for _ in range(3)],
            pltpu.VMEM((4, ROWS, CY), F32),
            dma((6,)),
            *[dma((FACES,)) for _ in range(4)],
            *[dma((blocks,)) for _ in range(6)],
        ],
        compiler_params=pltpu.CompilerParams(
            collective_id=0, has_side_effects=True, vmem_limit_bytes=40 * 2**20
        ),
    )(*in_hbm)
    return pl.pallas_call(
        second_kernel,
        name="second_sweeps",
        out_shape=[
            jax.ShapeDtypeStruct((CX, CY, CZ), F32),
            jax.ShapeDtypeStruct((FD, FW, FH), F32),
        ],
        in_specs=[vmem] * 7,
        out_specs=[anywhere] * 2,
        scratch_shapes=[
            pltpu.VMEM((CX, CY, CZ), F32),
            dma((PAIRS,)),
            dma,
        ],
        compiler_params=pltpu.CompilerParams(vmem_limit_bytes=40 * 2**20),
    )(*middle)


def solution(mesh):
    in_specs = (
        P("gx", "gy", "grp"),
        P("gx", "gy", "grp"),
        P("grp", "gx", "gy"),
        P("grp", "gx", "gy"),
        P("gx", "gy", None, None),
        P("gx", "gy", None),
    )
    out_specs = (P("gx", "gy", "grp"), P("grp", "gx", "gy"))
    sizes = (mesh.shape["grp"], mesh.shape["gx"])
    body = functools.partial(local, sizes)
    return jax.shard_map(body, mesh=mesh, in_specs=in_specs, out_specs=out_specs, check_vma=False)
```

```python
import functools

import jax
import jax.numpy as jnp
from jax import lax
from jax.experimental import pallas as pl
from jax.experimental.pallas import tpu as pltpu
from jax.sharding import PartitionSpec as P

F32 = jnp.float32
MESH = pl.DeviceIdType.MESH
DIAG = 7.0
SPECTRAL = 6.0 / DIAG
OMEGA = 1.0 / (1.0 - SPECTRAL * SPECTRAL / 2.0)
SEVENTH = 1.0 / 7.0

CX, CY, CZ = 16, 128, 256
FD, FW, FH = 64, 32, 256
ROWS = CX

HALF = CY // 2
PAIRS = CX // 2
CHUNK = 32

FLUID_UP, FLUID_DOWN, FLUID_SIDE = (0, 1), (2, 3), (4, 5)
FLUID_ABOVE, FLUID_BELOW = 6, 7
FIN_UP, FIN_DOWN, FIN_SIDE, FIN_ABOVE, FIN_BELOW = 8, 9, 10, 11, 12
FACES = 13


def iota(shape, axis):
    return lax.broadcasted_iota(jnp.int32, shape, axis)


def parity_rows(shape):
    rows, lanes = shape
    tile = (iota((8, lanes), 0) + iota((8, lanes), 1)) % 2
    return jnp.concatenate([tile] * (rows // 8), axis=0)


def shifted_rows(plane, low_tile, high_tile):
    rows, lanes = plane.shape
    sub = iota((8, lanes), 0)
    up = pltpu.roll(plane, 1, 0)
    down = pltpu.roll(plane, rows - 1, 0)
    up = jnp.concatenate([jnp.where(sub == 0, low_tile, up[:8]), up[8:]], axis=0)
    down = jnp.concatenate([down[:-8], jnp.where(sub == 7, high_tile, down[-8:])], axis=0)
    return up + down


def shifted_lanes(plane, low_tile, high_tile):
    rows, lanes = plane.shape
    lane = iota((rows, 128), 1)
    left = pltpu.roll(plane, 1, 1)
    right = pltpu.roll(plane, lanes - 1, 1)
    first = jnp.where(lane == 0, low_tile, left[:, :128]) + right[:, :128]
    last = left[:, 128:] + jnp.where(lane == 127, high_tile, right[:, 128:])
    return jnp.concatenate([first, last], axis=1)


def half_sweep(pair, source, target, active, side, low, high, red, core, put):
    x = 2 * pair
    for start in range(0, CY, CHUNK):
        rows = slice(start, start + CHUNK)
        even = parity_rows((CHUNK, CZ)) == 0
        here = source[pair + 1, rows]
        before, after = source[pair, rows], source[pair + 2, rows]
        near, far = active[x, rows], active[x + 1, rows]
        if red:
            total = here + jnp.where(even, before, after)
            on = jnp.where(even, near, far) == 1
        else:
            total = here + jnp.where(even, after, before)
            on = jnp.where(even, far, near) == 1
        if start == 0:
            low_tile = jnp.where(core == 1, pltpu.roll(side[pair], 1, 0), 0.0)
        else:
            low_tile = pltpu.roll(source[pair + 1, start - 8 : start], 1, 0)
        stop = start + CHUNK
        if stop == CY:
            high_tile = jnp.where(core == 0, pltpu.roll(side[pair], 7, 0), 0.0)
        else:
            high_tile = pltpu.roll(source[pair + 1, stop : stop + 8], 7, 0)
        total = total + shifted_rows(here, low_tile, high_tile)
        low_lane = pltpu.roll(low[rows], (128 - x) % 128, 1)
        high_lane = pltpu.roll(high[rows], 127 - x, 1)
        total = total + shifted_lanes(here, low_lane, high_lane)
        old = target[pair + 1, rows]
        put(rows, here, jnp.where(on, (old + total) * SEVENTH, old))


def fin_sum(group, k, field, low, high, side, core):
    d = group * 8 + k
    here = field[d + 1]
    total = field[d] + field[d + 2]
    low_tile = pltpu.roll(low[group], (8 - k) % 8, 0)
    high_tile = pltpu.roll(high[group], 7 - k, 0)
    total = total + shifted_rows(here, low_tile, high_tile)
    column = pltpu.roll(side[...], jnp.where(core == 1, (128 - d) % 128, 127 - d), 1)
    total = total + shifted_lanes(
        here, jnp.where(core == 1, column, 0.0), jnp.where(core == 0, column, 0.0)
    )
    return here, total


def pick_low(x, plane, low, rows=slice(None)):
    lane = iota((plane.shape[0], 128), 1)
    low[rows] = jnp.where(lane == x, pltpu.roll(plane[:, :128], x, 1), low[rows])


def pick_high(x, plane, high, rows=slice(None)):
    lane = iota((plane.shape[0], 128), 1)
    high[rows] = jnp.where(lane == x, pltpu.roll(plane[:, 128:], (x + 1) % 128, 1), high[rows])


def one_colour(plane, colour):
    folded = pltpu.roll(plane[HALF:], HALF - 1, 0)
    return jnp.where(parity_rows(folded.shape) == colour, plane[:HALF], folded)


def both_halves(folded):
    return jnp.concatenate([folded, pltpu.roll(folded, 1, 0)], axis=0)


def as_rows(columns):
    return jnp.transpose(columns)[:ROWS]


def as_columns(rows):
    square = jnp.concatenate([rows, jnp.zeros((CY - ROWS, CY), F32)], axis=0)
    return jnp.transpose(square)


def pick_rows(k, plane, low, high):
    sub = iota((8, plane.shape[1]), 0)
    low = jnp.where(sub == k, pltpu.roll(plane[:8], k, 0), low)
    high = jnp.where(sub == k, pltpu.roll(plane[-8:], (k + 1) % 8, 0), high)
    return low, high


def pick_side(d, plane, out, core):
    lane = iota((plane.shape[0], 128), 1)
    half = jnp.where(core == 0, plane[:, 128:], plane[:, :128])
    turned = pltpu.roll(half, jnp.where(core == 0, (d + 1) % 128, d), 1)
    out[...] = jnp.where(lane == d, turned, out[...])


def spread(rows, columns, offset, axis):
    a, b = iota((rows, columns), axis), iota((rows, columns), 1 - axis)
    return jnp.where(a == 2 * b + offset, 1.0, 0.0).astype(F32)


def dot(a, b):
    return jnp.dot(a, b, precision=lax.Precision.HIGHEST, preferred_element_type=F32)


def exchange_kernel(
    sizes,
    fluid, active, fin, source, owner, target,
    red, black, active_v, base, side2, low2, high2,
    fluid_v, fin_v, first, source_v, owner_v, target_v,
    side1, low1, high1, fin_low1, fin_high1, fin_side1, fin_low2, fin_high2, fin_side2,
    out_fin_low1, out_fin_high1, out_fin_side1, out_fin_low2, out_fin_high2, out_fin_side2,
    low_column, high_column,
    out_low1, out_high1, in_low1, in_high1, out_low2, out_high2, in_low2, in_high2,
    out_up1, out_down1, in_up1, in_down1, out_up2, out_down2, in_up2, in_down2,
    wall_out, wall_in, temps_out, temps_in, back_out, back_in, surface,
    load_sem, send1, recv1, send2, recv2, wall_send, wall_recv, temps_send, temps_recv, back_send, back_recv,
):
    groups, blocks = sizes
    grp, gx, core = lax.axis_index("grp"), lax.axis_index("gx"), lax.axis_index("gy")
    has_low, has_high = gx > 0, gx < blocks - 1
    has_below, has_above = grp > 0, grp < groups - 1
    on_wall = grp == 0
    left, right = (grp, gx - 1, core), (grp, gx + 1, core)
    below, above = (grp - 1, gx, core), (grp + 1, gx, core)
    other = (grp, gx, 1 - core)

    def wrapped(index):
        return jnp.where(index >= blocks, index - blocks, index)

    def peer(k):
        return (grp, wrapped(gx + k), core)

    def peer_back(k):
        return (grp, wrapped(gx - k + blocks), core)

    load_owner = pltpu.make_async_copy(owner, owner_v, load_sem.at[0])
    load_target = pltpu.make_async_copy(target, target_v, load_sem.at[1])
    load_fin = pltpu.make_async_copy(fin, fin_v.at[pl.ds(1, FD)], load_sem.at[2])
    load_fluid = pltpu.make_async_copy(fluid, fluid_v, load_sem.at[3])
    load_source = pltpu.make_async_copy(source, source_v, load_sem.at[4])
    load_active = pltpu.make_async_copy(active, active_v, load_sem.at[5])
    loads = (load_owner, load_target, load_fin, load_fluid, load_source, load_active)
    for load in loads:
        load.start()

    barrier = pltpu.get_barrier_semaphore()

    def greet(device):
        pl.semaphore_signal(barrier, inc=1, device_id=device, device_id_type=MESH)

    greet(other)

    @pl.when(has_above)
    def _():
        greet(above)

    @pl.when(has_below)
    def _():
        greet(below)

    @pl.when(on_wall)
    def _():
        def step(k, carry):
            greet(peer(k))
            return carry

        lax.fori_loop(1, blocks, step, 0)

    @pl.when(jnp.logical_not(on_wall) & has_low)
    def _():
        greet(left)

    @pl.when(jnp.logical_not(on_wall) & has_high)
    def _():
        greet(right)

    @pl.when(jnp.logical_not(has_low))
    def _():
        black[0] = jnp.zeros((CY, CZ), F32)
        red[0] = jnp.zeros((CY, CZ), F32)
        fin_low1[...] = jnp.zeros(fin_low1.shape, F32)
        fin_low2[...] = jnp.zeros(fin_low2.shape, F32)

    @pl.when(jnp.logical_not(has_high))
    def _():
        black[PAIRS + 1] = jnp.zeros((CY, CZ), F32)
        red[PAIRS + 1] = jnp.zeros((CY, CZ), F32)
        fin_high1[...] = jnp.zeros(fin_high1.shape, F32)
        fin_high2[...] = jnp.zeros(fin_high2.shape, F32)

    @pl.when(jnp.logical_not(has_below))
    def _():
        in_low1[...] = jnp.zeros(in_low1.shape, F32)

    @pl.when(jnp.logical_not(has_above))
    def _():
        in_high1[...] = jnp.zeros(in_high1.shape, F32)
        in_high2[...] = jnp.zeros(in_high2.shape, F32)
        fin_v[FD + 1] = jnp.zeros((FW, FH), F32)
        first[FD + 1] = jnp.zeros((FW, FH), F32)

    for ref in (low_column, high_column, out_fin_side1, out_fin_side2):
        ref[...] = jnp.zeros(ref.shape, F32)

    load_fin.wait()

    def pack_fin(group, carry):
        low = high = jnp.zeros((8, FH), F32)
        for k in range(8):
            plane = fin_v[group * 8 + k + 1]
            low, high = pick_rows(k, plane, low, high)
            pick_side(group * 8 + k, plane, out_fin_side1, core)
        out_fin_low1[group] = low
        out_fin_high1[group] = high
        return carry

    lax.fori_loop(0, FD // 8, pack_fin, 0)
    load_owner.wait()
    load_target.wait()

    expected = 1 + has_above.astype(jnp.int32) + has_below.astype(jnp.int32)
    sides = has_low.astype(jnp.int32) + has_high.astype(jnp.int32)
    pl.semaphore_wait(barrier, expected + jnp.where(on_wall, blocks - 1, sides))

    def link(src, dst, send, recv, k, device):
        return pltpu.make_async_remote_copy(
            src_ref=src, dst_ref=dst, send_sem=send.at[k], recv_sem=recv.at[k],
            device_id=device, device_id_type=MESH,
        )

    def wall_link(k):
        return link(wall_out.at[k], wall_in.at[k], wall_send, wall_recv, k, peer(k))

    def back_link(k):
        return link(back_out.at[k], back_in.at[k], back_send, back_recv, k, peer_back(k))

    def temps_link(k):
        return link(temps_out, temps_in.at[k], temps_send, temps_recv, k, peer(k))

    @pl.when(on_wall)
    def _():
        owners = owner_v[...]
        targets = target_v[...].astype(F32)

        def owned_by(k):
            return jnp.where(owners == wrapped(gx + k), targets, -1.0)

        def step(k, carry):
            wall_out[k] = owned_by(k)
            wall_link(k).start()
            return carry

        wall_in[0] = owned_by(0)
        lax.fori_loop(1, blocks, step, 0)

    side_row = pl.multiple_of(jnp.where(core == 0, CY - 8, 0), 8)

    def faces(send, recv, side_from, out_up, in_up, out_down, in_down, side, out_low, in_low, out_high, in_high,
              fin_from, fin_to, fin_low, fin_high, fin_side, sent_fin_low, sent_fin_high, sent_fin_side):
        links = {
            FLUID_ABOVE: (link(out_high, in_low, send, recv, FLUID_ABOVE, above), has_above, has_below),
            FLUID_BELOW: (link(out_low, in_high, send, recv, FLUID_BELOW, below), has_below, has_above),
            FIN_UP: (link(sent_fin_high, fin_low, send, recv, FIN_UP, right), has_high, has_low),
            FIN_DOWN: (link(sent_fin_low, fin_high, send, recv, FIN_DOWN, left), has_low, has_high),
            FIN_SIDE: (link(sent_fin_side, fin_side, send, recv, FIN_SIDE, other), None, None),
            FIN_ABOVE: (link(fin_from.at[FD], fin_to.at[0], send, recv, FIN_ABOVE, above), has_above, has_below),
            FIN_BELOW: (link(fin_from.at[1], fin_to.at[FD + 1], send, recv, FIN_BELOW, below), has_below, has_above),
        }
        for half in range(2):
            up, down, across = FLUID_UP[half], FLUID_DOWN[half], FLUID_SIDE[half]
            lanes = pl.ds(half * 128, 128)
            rim = side_from.at[pl.ds(1, PAIRS), pl.ds(side_row, 8), lanes]
            links[up] = (link(out_up.at[half], in_up.at[half], send, recv, up, right), has_high, has_low)
            links[down] = (link(out_down.at[half], in_down.at[half], send, recv, down, left), has_low, has_high)
            links[across] = (link(rim, side.at[:, :, lanes], send, recv, across, other), None, None)
        return links

    def when(condition, action):
        if condition is None:
            action()
        else:
            pl.when(condition)(action)

    one = faces(send1, recv1, black, out_up1, in_up1, out_down1, in_down1, side1, out_low1, in_low1, out_high1, in_high1,
                fin_v, fin_v, fin_low1, fin_high1, fin_side1, out_fin_low1, out_fin_high1, out_fin_side1)
    two = faces(send2, recv2, red, out_up2, in_up2, out_down2, in_down2, side2, out_low2, in_low2, out_high2, in_high2,
                first, first, fin_low2, fin_high2, fin_side2, out_fin_low2, out_fin_high2, out_fin_side2)

    def start(links, *which):
        for k in which:
            when(links[k][1], links[k][0].start)

    def arrived(links, *which):
        for k in which:
            when(links[k][2], links[k][0].wait_recv)

    def sent(links):
        for k in range(FACES):
            when(links[k][1], links[k][0].wait_send)

    start(one, FIN_SIDE, FIN_UP, FIN_DOWN, FIN_ABOVE, FIN_BELOW)

    load_fluid.wait()

    def pack_fluid(pair, carry):
        x = 2 * pair
        for start in range(0, CY, CHUNK):
            rows = slice(start, start + CHUNK)
            even = parity_rows((CHUNK, CZ)) == 0
            near, far = fluid_v[x, rows], fluid_v[x + 1, rows]
            reds, blacks = jnp.where(even, near, far), jnp.where(even, far, near)
            red[pair + 1, rows] = reds
            black[pair + 1, rows] = blacks
            pick_low(x, blacks, low_column, rows)
            pick_low(x + 1, reds, low_column, rows)
            pick_high(x, blacks, high_column, rows)
        return carry

    lax.fori_loop(0, PAIRS, pack_fluid, 0)
    out_low1[...] = as_rows(low_column[...])
    out_high1[...] = as_rows(high_column[...])

    def fold(field, pair, colour, out, half):
        out[half] = one_colour(field[pair + 1, :, half * 128 : half * 128 + 128], colour)

    for half in range(2):
        fold(black, PAIRS - 1, 0, out_up1, half)
        fold(black, 0, 1, out_down1, half)

    start(one, *FLUID_UP, *FLUID_DOWN, *FLUID_SIDE, FLUID_ABOVE, FLUID_BELOW)

    @pl.when(on_wall)
    def _():
        mixed = out_low1[...]
        swapped = jnp.where(
            iota(mixed.shape, 0) % 2 == 0, pltpu.roll(mixed, ROWS - 1, 0), pltpu.roll(mixed, 1, 0)
        )
        temps = jnp.where(iota(mixed.shape, 1) % 2 == 0, swapped, mixed)
        temps_out[...] = temps
        temps_in[0] = temps

        def step(k, carry):
            temps_link(k).start()
            return carry

        lax.fori_loop(1, blocks, step, 0)

    cells = (ROWS, CY)
    shifts = (0.0, 1.0, float(FH), float(FH + 1))

    def offsets(k):
        return wall_in[k] - (2 * FH * iota(cells, 0) + 2 * iota(cells, 1)).astype(F32)

    @pl.when(on_wall)
    def _():
        roots = fin_v[1]
        columns = [dot(roots, spread(FH, CY, dj, 0)) for dj in range(2)]
        for di in range(2):
            for dj in range(2):
                surface[2 * di + dj] = dot(spread(ROWS, FW, di, 1), columns[dj])

        def answer(k):
            offset = offsets(k)
            value = jnp.zeros(cells, F32)
            for n, shift in enumerate(shifts):
                value = jnp.where(offset == shift, surface[n], value)
            back_out[k] = value

        def step(k, carry):
            wall_link(k).wait_recv()
            answer(k)
            back_link(k).start()
            return carry

        answer(0)
        lax.fori_loop(1, blocks, step, 0)

    load_source.wait()
    arrived(one, FIN_SIDE, FIN_UP, FIN_DOWN, FIN_BELOW, FIN_ABOVE)

    def fin_step(group, carry):
        low = high = jnp.zeros((8, FH), F32)
        for k in range(8):
            d = group * 8 + k
            here, total = fin_sum(group, k, fin_v, fin_low1, fin_high1, fin_side1, core)
            rhs = here + source_v[d]
            new = (rhs + total) * SEVENTH
            first[d + 1] = new
            base[d] = (OMEGA * SEVENTH) * rhs + (1.0 - OMEGA) * here
            low, high = pick_rows(k, new, low, high)
            pick_side(d, new, out_fin_side2, core)
        out_fin_low2[group] = low
        out_fin_high2[group] = high
        return carry

    lax.fori_loop(1, FD // 8, fin_step, 0)

    @pl.when(on_wall)
    def _():
        def owned(k, sums):
            offset = offsets(k)
            flux = temps_in[k] - back_out[k]
            return tuple(
                total + jnp.where(offset == shift, flux, 0.0) for shift, total in zip(shifts, sums)
            )

        def step(k, sums):
            temps_link(k).wait_recv()
            return owned(k, sums)

        sums = owned(0, (jnp.zeros(cells, F32),) * 4)
        sums = lax.fori_loop(1, blocks, step, sums)
        deposit = jnp.zeros((FW, FH), F32)
        for dj in range(2):
            rows = dot(spread(FW, ROWS, 0, 0), sums[dj]) + dot(spread(FW, ROWS, 1, 0), sums[2 + dj])
            deposit = deposit + dot(rows, spread(CY, FH, dj, 1))
        fin_v[0] = deposit
        first[0] = deposit

    fin_step(0, 0)
    start(two, FIN_UP, FIN_DOWN, FIN_SIDE, FIN_ABOVE, FIN_BELOW)

    load_active.wait()
    arrived(one, *FLUID_UP, *FLUID_DOWN, *FLUID_SIDE, FLUID_ABOVE, FLUID_BELOW)
    low1[...] = as_columns(in_low1[...])
    high1[...] = as_columns(in_high1[...])

    def red_step(pair, carry):
        def put(rows, sources, new):
            red[pair + 1, rows] = new
            pick_low(2 * pair, new, low_column, rows)
            pick_high(2 * pair, new, high_column, rows)

        half_sweep(pair, black, red, active_v, side1, low1, high1, True, core, put)
        return carry

    def unfold(arrived_up, arrived_down, field):
        def low_plane():
            for half in range(2):
                field[0, :, half * 128 : half * 128 + 128] = both_halves(arrived_up[half])

        def high_plane():
            for half in range(2):
                field[PAIRS + 1, :, half * 128 : half * 128 + 128] = both_halves(arrived_down[half])

        when(has_low, low_plane)
        when(has_high, high_plane)

    unfold(in_up1, in_down1, black)
    lax.fori_loop(0, PAIRS, red_step, 0)
    out_low2[...] = as_rows(low_column[...])
    out_high2[...] = as_rows(high_column[...])
    fold(red, PAIRS - 1, 1, out_up2, 1)
    fold(red, 0, 0, out_down2, 1)
    start(two, FLUID_UP[1], FLUID_DOWN[1], FLUID_SIDE[1], FLUID_ABOVE, FLUID_BELOW)

    @pl.when(on_wall)
    def _():
        def step(k, total):
            back_link(k).wait_recv()
            return total + back_in[k]

        ghost = lax.fori_loop(1, blocks, step, back_out[0])
        later = pltpu.roll(ghost, ROWS - 1, 0)
        even_cell = iota(ghost.shape, 1) % 2 == 0
        in_low2[...] = jnp.where(even_cell, later, ghost)
        low2[...] = as_columns(jnp.where(even_cell, ghost, later))

        def fix(pair, carry):
            x = 2 * pair
            lane = iota((CY, 128), 1)
            even = parity_rows((CY, 128)) == 0
            on = jnp.where(even, active_v[x, :, :128], active_v[x + 1, :, :128]) == 1
            share = pltpu.roll(low2[...], (128 - x) % 128, 1) * SEVENTH
            half = red[pair + 1, :, :128]
            red[pair + 1, :, :128] = half + jnp.where(on & (lane == 0), share, 0.0)
            return carry

        lax.fori_loop(0, PAIRS, fix, 0)

    fold(red, PAIRS - 1, 1, out_up2, 0)
    fold(red, 0, 0, out_down2, 0)
    start(two, FLUID_UP[0], FLUID_DOWN[0], FLUID_SIDE[0])

    arrived(two, FIN_UP, FIN_DOWN, FIN_SIDE, FIN_ABOVE, FIN_BELOW)

    def fin_again(group, carry):
        for k in range(8):
            d = group * 8 + k
            _, total = fin_sum(group, k, first, fin_low2, fin_high2, fin_side2, core)
            base[d] = base[d] + (OMEGA * SEVENTH) * total
        return carry

    lax.fori_loop(0, FD // 8, fin_again, 0)

    sent(one)

    @pl.when(on_wall)
    def _():
        def step(k, carry):
            wall_link(k).wait_send()
            temps_link(k).wait_send()
            back_link(k).wait_send()
            return carry

        lax.fori_loop(1, blocks, step, 0)

    arrived(two, *FLUID_UP, *FLUID_DOWN, *FLUID_SIDE, FLUID_ABOVE, FLUID_BELOW)
    low2[...] = as_columns(in_low2[...])
    high2[...] = as_columns(in_high2[...])
    unfold(in_up2, in_down2, red)
    sent(two)


def second_kernel(red, black, active, fin_new, side, low, high, fluid_out, fin_out, fluid_v, fluid_sem, fin_sem):
    core = lax.axis_index("gy")
    fin_copy = pltpu.make_async_copy(fin_new, fin_out, fin_sem)
    fin_copy.start()

    def fluid_copy(pair):
        planes = pl.ds(2 * pair, 2)
        return pltpu.make_async_copy(fluid_v.at[planes], fluid_out.at[planes], fluid_sem.at[pair])

    def black_step(pair, carry):
        def put(rows, reds, new):
            even = parity_rows(new.shape) == 0
            fluid_v[2 * pair, rows] = jnp.where(even, reds, new)
            fluid_v[2 * pair + 1, rows] = jnp.where(even, new, reds)

        half_sweep(pair, red, black, active, side, low, high, False, core, put)
        fluid_copy(pair).start()
        return carry

    lax.fori_loop(0, PAIRS, black_step, 0)

    def done(pair, carry):
        fluid_copy(pair).wait()
        return carry

    lax.fori_loop(0, PAIRS, done, 0)
    fin_copy.wait()


def local(sizes, fluid_temp, active, fin_temp, fin_source, wall_owner, wall_target):
    blocks = sizes[1]
    owner = wall_owner.reshape(CX, CY)
    target = wall_target.reshape(CX, CY)
    anywhere = pl.BlockSpec(memory_space=pl.ANY)
    vmem = pl.BlockSpec(memory_space=pltpu.VMEM)
    column, rows, strip = (CY, 128), (FD // 8, 8, FH), (FW, 128)
    packed, rim = (PAIRS + 2, CY, CZ), (PAIRS, 8, CZ)
    held = [
        pltpu.VMEM(packed, F32),
        pltpu.VMEM(packed, F32),
        pltpu.VMEM((CX, CY, CZ), jnp.int32),
        *[pltpu.VMEM(s, F32) for s in ((FD, FW, FH), rim, column, column)],
    ]
    dma = pltpu.SemaphoreType.DMA
    in_hbm = [
        pltpu.with_memory_space_constraint(x, pltpu.HBM)
        for x in (fluid_temp, active, fin_temp, fin_source, owner, target)
    ]
    middle = pl.pallas_call(
        functools.partial(exchange_kernel, sizes),
        name="exchange_and_first_sweeps",
        out_shape=held,
        in_specs=[anywhere] * 6,
        out_specs=[vmem] * 7,
        scratch_shapes=[
            pltpu.VMEM((CX, CY, CZ), F32),
            pltpu.VMEM((FD + 2, FW, FH), F32),
            pltpu.VMEM((FD + 2, FW, FH), F32),
            pltpu.VMEM((FD, FW, FH), F32),
            pltpu.VMEM((CX, CY), jnp.int32),
            pltpu.VMEM((CX, CY), jnp.int32),
            *[pltpu.VMEM(s, F32) for s in (rim, column, column, rows, rows, strip)],
            *[pltpu.VMEM(s, F32) for s in (rows, rows, strip)],
            *[pltpu.VMEM(s, F32) for s in (rows, rows, strip)],
            *[pltpu.VMEM(s, F32) for s in (rows, rows, strip)],
            *[pltpu.VMEM(column, F32) for _ in range(2)],
            *[pltpu.VMEM((ROWS, CY), F32) for _ in range(8)],
            *[pltpu.VMEM((2, HALF, 128), F32) for _ in range(8)],
            pltpu.VMEM((blocks, ROWS, CY), F32),
            pltpu.VMEM((blocks, ROWS, CY), F32),
            pltpu.VMEM((ROWS, CY), F32),
            *[pltpu.VMEM((blocks, ROWS, CY), F32) for _ in range(3)],
            pltpu.VMEM((4, ROWS, CY), F32),
            dma((6,)),
            *[dma((FACES,)) for _ in range(4)],
            *[dma((blocks,)) for _ in range(6)],
        ],
        compiler_params=pltpu.CompilerParams(
            collective_id=0, has_side_effects=True, vmem_limit_bytes=40 * 2**20
        ),
    )(*in_hbm)
    return pl.pallas_call(
        second_kernel,
        name="second_sweeps",
        out_shape=[
            jax.ShapeDtypeStruct((CX, CY, CZ), F32),
            jax.ShapeDtypeStruct((FD, FW, FH), F32),
        ],
        in_specs=[vmem] * 7,
        out_specs=[anywhere] * 2,
        scratch_shapes=[
            pltpu.VMEM((CX, CY, CZ), F32),
            dma((PAIRS,)),
            dma,
        ],
        compiler_params=pltpu.CompilerParams(vmem_limit_bytes=40 * 2**20),
    )(*middle)


def solution(mesh):
    in_specs = (
        P("gx", "gy", "grp"),
        P("gx", "gy", "grp"),
        P("grp", "gx", "gy"),
        P("grp", "gx", "gy"),
        P("gx", "gy", None, None),
        P("gx", "gy", None),
    )
    out_specs = (P("gx", "gy", "grp"), P("grp", "gx", "gy"))
    sizes = (mesh.shape["grp"], mesh.shape["gx"])
    body = functools.partial(local, sizes)
    return jax.shard_map(body, mesh=mesh, in_specs=in_specs, out_specs=out_specs, check_vma=False)
```
